512 devices in a mesh: row: 8 (over z), col: 16 (over y, core), rep: 4 (over x).
Axes of the slice: x: 4, y: 8, z: 8, core: 2. Of those that a mesh axis runs over, the one named last changes fastest.
Arguments:
- tile_values: bfloat16 [8, 16, 96, 128, 128], P('row', 'col'), may hold values from -0.078125 to 0.078125
- tile_rows: int32 [8, 16, 96], P('row', 'col'), may hold values from 0 to 31, as said below
- tile_cols: int32 [8, 16, 96], P('row', 'col'), may hold values from 0 to 15, as said below
- tile_count: int32 [8, 16], P('row', 'col'), may hold values from 24 to 96, as said below
- features: bfloat16 [32768, 512], P('col', 'rep'), may hold values from -6 to 6
- weight: bfloat16 [512, 512], P('rep'), may hold values from -0.25 to 0.25
- cotangent: bfloat16 [32768, 512], P(('row', 'col')), may hold values from -6 to 6
Outputs:
- activation: bfloat16 [32768, 512], P(('row', 'col'))
- weight_grad: float32 [512, 512], P('rep')
- input_grad: bfloat16 [32768, 512], P('col', 'rep')
The draws below stay inside these ranges and needn't reach their ends.
Inputs may be any that keep to these rules, and one draw needn't show every extreme that they name: Row blocks lie below 32; within one grid block the slots hold distinct (tile_rows, tile_cols) pairs. `tile_cols`: column blocks lie below 16. `tile_count`: slots at or beyond a block's count hold no tile; some grid block uses all 96 slots.
All inputs are finite; a program needn't handle non-finite values.
Results may differ from the reference program's by a relative error of at most 0.006.
Values may be sent and summed in bfloat16 or wider, within the bound.
No kernel may reach another device: no remote copies, remote signals or barrier semaphores. Data moves between devices by JAX's collectives and lax.ppermute only.
A program may use at most 64 MiB of HBM per device.

```python
import math
import jax
import jax.numpy as jnp
from jax import lax

F = 512
TB = 128
CH = 256
TILES = 96
ROW_NODES = 4096
COL_NODES = 2048
NODES = 32768
N_ROW = 8
N_COL = 16


def tile_pairs(key):
    block_pairs = N_COL * CH // TB * (N_ROW * CH // TB)
    keys = jax.random.split(jax.random.fold_in(key, 11), N_ROW * N_COL)

    def one_block(block_key):
        return jax.random.permutation(block_key, block_pairs)[:TILES].astype(jnp.int32)
    pairs = jax.vmap(one_block)(keys)
    return pairs.reshape(N_ROW, N_COL, TILES)


def draw_tile_rows(key, part):
    pairs = tile_pairs(key)
    return (pairs // (N_ROW * CH // TB)).astype(jnp.int32)


def draw_tile_cols(key, part):
    pairs = tile_pairs(key)
    return (pairs % (N_ROW * CH // TB)).astype(jnp.int32)


def draw_tile_count(key, part):
    key = jax.random.fold_in(key, 5)
    first, second = jax.random.split(key)
    lowest = max(TILES // 4, 1)
    counts = jax.random.randint(first, (N_ROW * N_COL,), lowest, TILES + 1).astype(jnp.int32)
    fullest = jax.random.randint(second, (), 0, N_ROW * N_COL).astype(jnp.int32)
    counts = jnp.where(jnp.arange(N_ROW * N_COL, dtype=jnp.int32) == fullest, TILES, counts)
    return counts.reshape(N_ROW, N_COL).astype(jnp.int32)


def level_of(stream_key, shape, cuts, low, top_value):
    def one(axis_at, parts):
        draws = jax.random.uniform(jax.random.fold_in(jax.random.fold_in(stream_key, 6), axis_at), (parts,), jnp.float32, low / len(cuts), top_value / len(cuts))
        return jnp.repeat(jnp.exp(draws), shape[axis_at] // parts).reshape((-1,) + (1,) * (len(shape) - axis_at - 1))

    loudness = one(*cuts[0])
    for cut in cuts[1:]:
        loudness = loudness * one(*cut)
    return loudness


def gaussian(own_key, extent, scale, limit, cuts=(), kind=jnp.bfloat16):
    entries = scale * jax.random.normal(own_key, extent, jnp.float32)
    if cuts:
        entries = entries * level_of(own_key, extent, cuts, -0.22, 0.18)
    return jnp.clip(entries, -limit, limit).astype(kind)


def setup_inputs(seed: int = 0) -> dict:
    key_list = jax.random.split(jax.random.key(seed), 8)
    tile_values = gaussian(key_list[0], (N_ROW, N_COL, TILES, TB, TB), (TILES * TB * TB // CH) ** -0.5, 0.078125, ((0, 8), (1, 16)))
    tile_rows = draw_tile_rows(jax.random.fold_in(key_list[7], 71), 0)
    tile_cols = draw_tile_cols(jax.random.fold_in(key_list[7], 71), 0)
    tile_count = draw_tile_count(jax.random.fold_in(key_list[7], 71), 0)
    features = gaussian(key_list[4], (NODES, F), 1.0, 6.0, ((0, 16), (1, 4)))
    weight = gaussian(key_list[5], (F, F), F ** -0.5, 0.25, ((0, 4),))
    cotangent = gaussian(key_list[6], (NODES, F), 1.0, 6.0, ((0, 128),))
    return dict(tile_values=tile_values, tile_rows=tile_rows, tile_cols=tile_cols, tile_count=tile_count, features=features, weight=weight, cotangent=cotangent)


def block_sum(select, contrib):
    return jnp.einsum('bt,tif->bif', select, contrib, precision=lax.Precision.HIGHEST)

def reference(tile_values, tile_rows, tile_cols, tile_count, features, weight, cotangent):
    row_blocks = ROW_NODES // TB
    col_blocks = COL_NODES // TB
    slot_ids = jnp.arange(TILES, dtype=jnp.int32)

    def forward_row(r):

        def step(total, c):
            source = lax.dynamic_slice_in_dim(features, (c * COL_NODES).astype(jnp.int32), COL_NODES, 0)
            source = source.reshape(col_blocks, TB, F)
            picked = jnp.take(source, tile_cols[r, c], axis=0)
            contrib = jnp.einsum('tij,tjf->tif', tile_values[r, c].astype(jnp.float32), picked.astype(jnp.float32), precision=lax.Precision.HIGHEST)
            live = slot_ids < tile_count[r, c]
            select = ((tile_rows[r, c][None, :] == jnp.arange(row_blocks, dtype=jnp.int32)[:, None]) & live[None, :]).astype(jnp.float32)
            return (total + block_sum(select, contrib).reshape(ROW_NODES, F), None)
        total, _ = lax.scan(step, jnp.zeros((ROW_NODES, F), jnp.float32), jnp.arange(N_COL, dtype=jnp.int32))
        return total
    aggregated = lax.map(forward_row, jnp.arange(N_ROW, dtype=jnp.int32)).reshape(NODES, F).astype(jnp.bfloat16)
    hidden = jnp.dot(aggregated, weight, preferred_element_type=jnp.float32)
    sigma = jax.nn.sigmoid(hidden)
    activation = (hidden * sigma).astype(jnp.bfloat16)
    slope = sigma * (1.0 + hidden * (1.0 - sigma))
    grad_hidden = (cotangent.astype(jnp.float32) * slope).astype(jnp.bfloat16)
    weight_grad = lax.dot_general(aggregated, grad_hidden, (((0,), (0,)), ((), ())), preferred_element_type=jnp.float32) * (1.0 / math.sqrt(NODES))
    grad_agg = lax.dot_general(grad_hidden, weight, (((1,), (1,)), ((), ())), preferred_element_type=jnp.float32).astype(jnp.bfloat16)

    def backward_col(c):

        def step(total, r):
            source = lax.dynamic_slice_in_dim(grad_agg, (r * ROW_NODES).astype(jnp.int32), ROW_NODES, 0)
            source = source.reshape(row_blocks, TB, F)
            picked = jnp.take(source, tile_rows[r, c], axis=0)
            contrib = jnp.einsum('tji,tjf->tif', tile_values[r, c].astype(jnp.float32), picked.astype(jnp.float32), precision=lax.Precision.HIGHEST)
            live = slot_ids < tile_count[r, c]
            select = ((tile_cols[r, c][None, :] == jnp.arange(col_blocks, dtype=jnp.int32)[:, None]) & live[None, :]).astype(jnp.float32)
            return (total + block_sum(select, contrib).reshape(COL_NODES, F), None)
        total, _ = lax.scan(step, jnp.zeros((COL_NODES, F), jnp.float32), jnp.arange(N_ROW, dtype=jnp.int32))
        return total
    input_grad = lax.map(backward_col, jnp.arange(N_COL, dtype=jnp.int32)).reshape(NODES, F).astype(jnp.bfloat16)
    return (activation, weight_grad, input_grad)
```

```python
import functools
import math

import jax
import jax.numpy as jnp
from jax import lax
from jax.experimental import pallas as pl
from jax.experimental.pallas import tpu as pltpu
from jax.sharding import Mesh
from jax.sharding import PartitionSpec as P

VMEM_LIMIT = 40 * 1024 * 1024
CHUNK = 16
GROUP = 4
BF = jnp.bfloat16
F4 = jnp.float32

VMEM = pl.BlockSpec(memory_space=pltpu.VMEM)
SMEM = pl.BlockSpec(memory_space=pltpu.SMEM)
HBM = pl.BlockSpec(memory_space=pl.ANY)


def dot(a, b, dims=(((1,), (0,)), ((), ()))):
    return lax.dot_general(a, b, dims, preferred_element_type=F4)


def tile_copies(values, tiles, sems):
    return [
        pltpu.make_async_copy(
            values.at[pl.ds(first, CHUNK)], tiles.at[pl.ds(first, CHUNK)], sems.at[first // CHUNK]
        )
        for first in range(0, tiles.shape[0], CHUNK)
    ]


def walk_tiles(used, copies, out_ids, dump, product, acc):
    for chunk, copy in enumerate(copies):
        copy.wait()
        first = chunk * CHUNK
        groups = jnp.clip((used - first + GROUP - 1) // GROUP, 0, CHUNK // GROUP)

        @pl.loop(0, groups)
        def _(g):
            slots = [first + g * GROUP + u for u in range(GROUP)]
            terms = [product(t) for t in slots]
            for t, term in zip(slots, terms):
                place = jnp.where(t < used, out_ids[t], dump)
                acc[place] += term


def forward_kernel(row_ids, col_ids, count, core, values, feats, own, other, tiles, acc, sems):
    copies = tile_copies(values, tiles, sems)
    for copy in copies:
        copy.start()
    acc[...] = jnp.zeros_like(acc)

    def product(t):
        return dot(tiles[t], feats[col_ids[t]])

    walk_tiles(count[0], copies, row_ids, acc.shape[0] - 1, product, acc)
    ys, grains, _ = own.shape
    blocks = grains // acc.shape[1]
    me = core[0]
    for y in range(ys):
        for b in range(blocks):
            rows = pl.ds(b * acc.shape[1], acc.shape[1])
            own[y, rows, :] = acc[(2 * y + me) * blocks + b]
            other[y, rows, :] = acc[(2 * y + 1 - me) * blocks + b].astype(BF)


def forward_tiles(row_ids, col_ids, count, core, values, feats, ys, grains):
    slots, side, _ = values.shape
    width = feats.shape[-1]
    row_blocks = 2 * ys * grains // side
    return pl.pallas_call(
        forward_kernel,
        out_shape=(
            jax.ShapeDtypeStruct((ys, grains, width), F4),
            jax.ShapeDtypeStruct((ys, grains, width), BF),
        ),
        in_specs=[SMEM, SMEM, SMEM, SMEM, HBM, VMEM],
        out_specs=(VMEM, VMEM),
        scratch_shapes=[
            pltpu.VMEM((slots, side, side), BF),
            pltpu.VMEM((row_blocks + 1, side, width), F4),
            pltpu.SemaphoreType.DMA((slots // CHUNK,)),
        ],
        compiler_params=pltpu.CompilerParams(vmem_limit_bytes=VMEM_LIMIT),
        name="forward_tiles",
    )(row_ids, col_ids, count, core, values, feats)


def dense_kernel(aggs, own_agg, w_all, w_own, cot, act, payload):
    reps, grains, width = aggs.shape
    ys, _, side = payload.shape
    hidden = dot(aggs[0], w_all[pl.ds(0, width), :])
    for q in range(1, reps):
        hidden += dot(aggs[q], w_all[pl.ds(q * width, width), :])
    sigma = jax.nn.sigmoid(hidden)
    act[...] = (hidden * sigma).astype(BF)
    slope = sigma * (1.0 + hidden * (1.0 - sigma))
    grad_hidden = (cot[...].astype(F4) * slope).astype(BF)
    back = dot(w_own[...], grad_hidden, (((1,), (1,)), ((), ()))).astype(BF)
    share = dot(own_agg[...], grad_hidden, (((0,), (0,)), ((), ()))).astype(BF)
    part = width // ys
    for y in range(ys):
        for b in range(grains // side):
            payload[y, pl.ds(b * width, width), :] = back[:, b * side : (b + 1) * side]
        base = grains // side * width
        for k in range(share.shape[1] // side):
            payload[y, pl.ds(base + k * part, part), :] = share[
                y * part : (y + 1) * part, k * side : (k + 1) * side
            ]


def dense(aggs, own_agg, w_all, w_own, cot, ys, side):
    reps, grains, width = aggs.shape
    total = w_own.shape[1]
    rows = grains // side * width + width // ys * (total // side)
    return pl.pallas_call(
        dense_kernel,
        out_shape=(
            jax.ShapeDtypeStruct((grains, total), BF),
            jax.ShapeDtypeStruct((ys, rows, side), BF),
        ),
        in_specs=[VMEM] * 5,
        out_specs=(VMEM, VMEM),
        compiler_params=pltpu.CompilerParams(vmem_limit_bytes=VMEM_LIMIT),
        name="dense",
    )(aggs, own_agg, w_all, w_own, cot)


def backward_kernel(
    row_ids, col_ids, count, core, values, mine, theirs, payload, tiles, grads, acc, sems, gsems
):
    me = core[0]
    copies = tile_copies(values, tiles, sems)
    take = [
        pltpu.make_async_copy(mine, grads.at[me], gsems.at[0]),
        pltpu.make_async_copy(theirs, grads.at[1 - me], gsems.at[1]),
    ]
    for copy in take + copies:
        copy.start()
    acc[...] = jnp.zeros_like(acc)
    side = tiles.shape[1]
    width = acc.shape[1]
    rows, _, _ = payload.shape
    ys = grads.shape[1]
    col_blocks = acc.shape[0] - 1
    per_row = col_blocks // rows
    blocks = per_row
    base = blocks * width
    for copy in take:
        copy.wait()

    def product(t):
        b = row_ids[t]
        device = b // blocks
        start = pl.multiple_of((b % blocks) * width, width)
        return dot(grads[device % 2, device // 2, pl.ds(start, width), :], tiles[t])

    share = jnp.zeros((payload.shape[1] - base, side), F4)
    for c in range(2):
        for y in range(ys):
            share += grads[c, y, base:, :].astype(F4)
    share = share.astype(BF)
    walk_tiles(count[0], copies, col_ids, col_blocks, product, acc)
    for r in range(rows):
        for b in range(per_row):
            payload[r, pl.ds(b * width, width), :] = acc[r * per_row + b].astype(BF)
        payload[r, base:, :] = share


def backward_tiles(row_ids, col_ids, count, core, values, mine, theirs, rows, col_blocks):
    slots, side, _ = values.shape
    ys, length, _ = mine.shape
    width = side
    return pl.pallas_call(
        backward_kernel,
        out_shape=jax.ShapeDtypeStruct((rows, length, side), BF),
        in_specs=[SMEM, SMEM, SMEM, SMEM, HBM, HBM, HBM],
        out_specs=VMEM,
        scratch_shapes=[
            pltpu.VMEM((slots, side, side), BF),
            pltpu.VMEM((2, ys, length, side), BF),
            pltpu.VMEM((col_blocks + 1, width, side), F4),
            pltpu.SemaphoreType.DMA((slots // CHUNK,)),
            pltpu.SemaphoreType.DMA((2,)),
        ],
        compiler_params=pltpu.CompilerParams(vmem_limit_bytes=VMEM_LIMIT),
        name="backward_tiles",
    )(row_ids, col_ids, count, core, values, mine, theirs)


def finish_kernel(scale, parts, grad, share):
    rows, length, side = parts.shape
    copies, grains, width = grad.shape
    base = grains // side * width
    total = parts[0].astype(F4)
    for r in range(1, rows):
        total += parts[r].astype(F4)
    for b in range(grains // side):
        block = total[b * width : (b + 1) * width].T.astype(BF)
        for r in range(copies):
            grad[r, pl.ds(b * side, side), :] = block
    ys, part, _ = share.shape
    for k in range(share.shape[2] // side):
        piece = total[base + k * part : base + (k + 1) * part] * scale
        for y in range(ys):
            share[y, :, k * side : (k + 1) * side] = piece


def finish(parts, scale, grains, width, ys, total):
    rows, length, side = parts.shape
    return pl.pallas_call(
        functools.partial(finish_kernel, scale),
        out_shape=(
            jax.ShapeDtypeStruct((rows, grains, width), BF),
            jax.ShapeDtypeStruct((ys, width // ys, total), F4),
        ),
        in_specs=[VMEM],
        out_specs=(VMEM, VMEM),
        compiler_params=pltpu.CompilerParams(vmem_limit_bytes=VMEM_LIMIT),
        name="finish",
    )(parts)


def swap_cores(x):
    return lax.ppermute(x, "core", [(0, 1), (1, 0)])


def exchange(x, axis):
    return lax.all_to_all(x, axis, 0, 0, tiled=True)


def body(tile_values, tile_rows, tile_cols, tile_count, features, weight, cotangent):
    values = tile_values[0, 0]
    row_ids = tile_rows[0, 0]
    col_ids = tile_cols[0, 0]
    count = tile_count[0]
    core = lax.axis_index("core").astype(jnp.int32).reshape(1)
    side = values.shape[-1]
    width = features.shape[1]
    grains, total = cotangent.shape
    ys, rows, reps = (lax.axis_size(a) for a in ("y", "row", "rep"))
    col_blocks = features.shape[0] // side
    nodes = grains * rows * ys * 2

    w_all = lax.all_gather(weight, "rep", axis=0, tiled=True)
    feats = features.reshape(col_blocks, side, width)
    own, other = forward_tiles(row_ids, col_ids, count, core, values, feats, ys, grains)
    pair = (own + swap_cores(other).astype(F4)).astype(BF)
    parts = exchange(pair, "y")
    agg = jnp.sum(parts.astype(F4), axis=0).astype(BF)
    aggs = lax.all_gather(agg, "rep", axis=0)
    activation, payload = dense(aggs, agg, w_all, weight, cotangent, ys, side)
    mine = exchange(payload, "y")
    theirs = swap_cores(mine)
    back = backward_tiles(row_ids, col_ids, count, core, values, mine, theirs, rows, col_blocks)
    sums = exchange(back, "row")
    grad, share = finish(sums, 1.0 / math.sqrt(nodes), grains, width, ys, total)
    input_grad = exchange(grad, "row").reshape(rows * grains, width)
    weight_grad = exchange(share, "y").reshape(width, total)
    return (activation, weight_grad, input_grad)


def solution(mesh):
    rows, cols, reps = mesh.devices.shape
    split = Mesh(
        mesh.devices.reshape(rows, cols // 2, 2, reps), ("row", "y", "core", "rep")
    )
    col = ("y", "core")
    return jax.shard_map(
        body,
        mesh=split,
        in_specs=(
            P("row", col, None, None, None),
            P("row", col, None),
            P("row", col, None),
            P("row", col),
            P(col, "rep"),
            P("rep", None),
            P(("row",) + col, None),
        ),
        out_specs=(P(("row",) + col, None), P("rep", None), P(col, "rep")),
        check_vma=False,
    )
```

```python
import functools
import math

import jax
import jax.numpy as jnp
from jax import lax
from jax.experimental import pallas as pl
from jax.experimental.pallas import tpu as pltpu
from jax.sharding import Mesh
from jax.sharding import PartitionSpec as P

VMEM_LIMIT = 40 * 1024 * 1024
FORWARD_VMEM = 51 * 1024 * 1024
CHUNK = 16
BF = jnp.bfloat16
F4 = jnp.float32

VMEM = pl.BlockSpec(memory_space=pltpu.VMEM)
SMEM = pl.BlockSpec(memory_space=pltpu.SMEM)
ANY = pl.BlockSpec(memory_space=pl.ANY)
HOLDERS = 4


def dot(a, b, dims=(((1,), (0,)), ((), ()))):
    return lax.dot_general(a, b, dims, preferred_element_type=F4)


def tile_copies(values, tiles, sems):
    return [
        pltpu.make_async_copy(
            values.at[pl.ds(first, CHUNK)], tiles.at[pl.ds(first, CHUNK)], sems.at[first // CHUNK]
        )
        for first in range(0, tiles.shape[0], CHUNK)
    ]


def pack_ids(row_ids, col_ids, used, row_blocks, col_blocks):
    live = jnp.arange(row_ids.shape[0], dtype=jnp.int32) < used
    span = 2 * col_blocks
    return jnp.where(live, row_ids * span + col_ids, row_blocks * span + col_blocks)


def forward_kernel(
    core, ids_any, values, feats_any, own, other, ids, feats, tiles, acc, sems, more_sems
):
    first = [
        pltpu.make_async_copy(ids_any, ids, more_sems.at[0]),
        pltpu.make_async_copy(feats_any, feats, more_sems.at[1]),
    ]
    copies = tile_copies(values, tiles, sems)
    for copy in first + copies:
        copy.start()
    acc[...] = jnp.zeros_like(acc)
    for copy in first:
        copy.wait()
    col_blocks, side, _ = feats.shape
    for chunk, copy in enumerate(copies):
        copy.wait()
        for t in range(chunk * CHUNK, (chunk + 1) * CHUNK):
            acc[ids[t] // (2 * col_blocks)] += dot(tiles[t], feats[ids[t] % col_blocks])
    ys, grains, _ = own.shape
    blocks = grains // side
    me = core[0]
    for y in range(ys):
        for b in range(blocks):
            rows = pl.ds(b * side, side)
            own[y, rows, :] = acc[(2 * y + me) * blocks + b]
            other[y, rows, :] = acc[(2 * y + 1 - me) * blocks + b].astype(BF)


def forward_tiles(core, ids, values, feats, ys, grains):
    slots, side, _ = values.shape
    width = feats.shape[-1]
    row_blocks = 2 * ys * grains // side
    return pl.pallas_call(
        forward_kernel,
        out_shape=(
            jax.ShapeDtypeStruct((ys, grains, width), F4),
            jax.ShapeDtypeStruct((ys, grains, width), BF),
        ),
        in_specs=[SMEM, ANY, ANY, ANY],
        out_specs=(VMEM, VMEM),
        scratch_shapes=[
            pltpu.SMEM(ids.shape, jnp.int32),
            pltpu.VMEM(feats.shape, BF),
            pltpu.VMEM((slots, side, side), BF),
            pltpu.VMEM((row_blocks + 1, side, width), F4),
            pltpu.SemaphoreType.DMA((slots // CHUNK,)),
            pltpu.SemaphoreType.DMA((2,)),
        ],
        compiler_params=pltpu.CompilerParams(vmem_limit_bytes=FORWARD_VMEM),
        name="forward_tiles",
    )(core, ids, values, feats)


def pair_kernel(own, theirs, weight, pair, lent):
    pair[...] = (own[...] + theirs[...].astype(F4)).astype(BF)
    lent[...] = weight[...]


def add_pair(own, theirs, weight):
    return pl.pallas_call(
        pair_kernel,
        out_shape=(
            jax.ShapeDtypeStruct(own.shape, BF),
            jax.ShapeDtypeStruct(weight.shape, BF),
        ),
        in_specs=[VMEM] * 3,
        out_specs=(VMEM, VMEM),
        compiler_params=pltpu.CompilerParams(vmem_limit_bytes=VMEM_LIMIT),
        name="add_pair",
    )(own, theirs, weight)


def fold_kernel(parts, *refs):
    copies = refs[-1]
    total = parts[0].astype(F4)
    for y in range(1, parts.shape[0]):
        total += parts[y].astype(F4)
    total = total.astype(BF)
    for q in range(copies.shape[0]):
        copies[q] = total


def fold(parts, copies, before):
    return pl.pallas_call(
        fold_kernel,
        out_shape=jax.ShapeDtypeStruct((copies,) + parts.shape[1:], BF),
        in_specs=[VMEM] + [ANY] * len(before),
        out_specs=VMEM,
        compiler_params=pltpu.CompilerParams(vmem_limit_bytes=VMEM_LIMIT),
        name="fold",
    )(parts, *before)


def dense_kernel(rep, aggs, own_weight, *refs):
    reps, grains, width = aggs.shape
    others, (cot, act, payload) = refs[: reps - 1], refs[reps - 1 :]
    me = rep[0]
    ys, _, side = payload.shape
    own_agg = aggs[me]
    hidden = dot(own_agg, own_weight[...])
    for k, weight in enumerate(others):
        hidden += dot(aggs[(me + k + 1) % reps], weight[...])
    sigma = jax.nn.sigmoid(hidden)
    act[...] = (hidden * sigma).astype(BF)
    slope = sigma * (1.0 + hidden * (1.0 - sigma))
    grad_hidden = (cot[...].astype(F4) * slope).astype(BF)
    back = dot(own_weight[...], grad_hidden, (((1,), (1,)), ((), ()))).astype(BF)
    share = dot(own_agg, grad_hidden, (((0,), (0,)), ((), ()))).astype(BF)
    holders = min(HOLDERS, ys)
    part = width // holders
    base = grains // side * width
    for y in range(ys):
        for b in range(grains // side):
            payload[y, pl.ds(b * width, width), :] = back[:, b * side : (b + 1) * side]
        chunk = y % holders
        for k in range(share.shape[1] // side):
            payload[y, pl.ds(base + k * part, part), :] = share[
                chunk * part : (chunk + 1) * part, k * side : (k + 1) * side
            ]


def dense(rep, aggs, weights, cot, ys, side):
    reps, grains, width = aggs.shape
    total = cot.shape[1]
    rows = grains // side * width + width // min(HOLDERS, ys) * (total // side)
    return pl.pallas_call(
        dense_kernel,
        out_shape=(
            jax.ShapeDtypeStruct((grains, total), BF),
            jax.ShapeDtypeStruct((ys, rows, side), BF),
        ),
        in_specs=[SMEM] + [VMEM] * (reps + 2),
        out_specs=(VMEM, VMEM),
        compiler_params=pltpu.CompilerParams(vmem_limit_bytes=VMEM_LIMIT),
        name="dense",
    )(rep, aggs, *weights, cot)


def backward_kernel(ids, core, tiles, mine, theirs, payload, acc):
    acc[...] = jnp.zeros_like(acc)
    side = tiles.shape[1]
    width = acc.shape[1]
    rows = payload.shape[0]
    ys = mine.shape[0]
    col_blocks = acc.shape[0] - 1
    per_row = col_blocks // rows
    base = per_row * width

    for t in range(tiles.shape[0]):
        b = ids[t] // (2 * col_blocks) % (2 * ys * per_row)
        device = b // per_row
        block = pl.ds(pl.multiple_of((b % per_row) * width, width), width)
        grad = jnp.where(device % 2 == core[0], mine[device // 2, block], theirs[device // 2, block])
        acc[ids[t] % (2 * col_blocks)] += dot(grad, tiles[t])
    share = jnp.zeros((payload.shape[1] - base, side), F4)
    for grads in (mine, theirs):
        for y in range(ys):
            share += grads[y, base:, :].astype(F4)
    share = share.astype(BF)
    for r in range(rows):
        for b in range(per_row):
            payload[r, pl.ds(b * width, width), :] = acc[r * per_row + b].astype(BF)
        payload[r, base:, :] = share


def backward_tiles(ids, core, values, mine, theirs, rows, col_blocks):
    side = values.shape[1]
    length = mine.shape[1]
    return pl.pallas_call(
        backward_kernel,
        out_shape=jax.ShapeDtypeStruct((rows, length, side), BF),
        in_specs=[SMEM] * 2 + [VMEM] * 3,
        out_specs=VMEM,
        scratch_shapes=[pltpu.VMEM((col_blocks + 1, side, side), F4)],
        compiler_params=pltpu.CompilerParams(vmem_limit_bytes=VMEM_LIMIT),
        name="backward_tiles",
    )(ids, core, values, mine, theirs)


def finish_kernel(scale, parts, grad, share):
    rows, length, side = parts.shape
    width = side
    grains = grad.shape[0] // rows
    base = grains // side * width
    total = parts[0].astype(F4)
    for r in range(1, rows):
        total += parts[r].astype(F4)
    for b in range(grains // side):
        block = total[b * width : (b + 1) * width].T.astype(BF)
        for r in range(rows):
            grad[pl.ds(r * grains + b * side, side), :] = block
    part = share.shape[0]
    for k in range(share.shape[1] // side):
        share[:, k * side : (k + 1) * side] = total[base + k * part : base + (k + 1) * part] * scale


def finish(parts, scale, grains, part, total):
    rows, length, side = parts.shape
    return pl.pallas_call(
        functools.partial(finish_kernel, scale),
        out_shape=(
            jax.ShapeDtypeStruct((rows * grains, side), BF),
            jax.ShapeDtypeStruct((part, total), F4),
        ),
        in_specs=[VMEM],
        out_specs=(VMEM, VMEM),
        compiler_params=pltpu.CompilerParams(vmem_limit_bytes=VMEM_LIMIT),
        name="finish",
    )(parts)


def fetch_others(weight):
    reps = lax.axis_size("rep")
    if reps != 4:
        return [
            lax.ppermute(weight, "rep", [((i + k) % reps, i) for i in range(reps)])
            for k in range(1, reps)
        ]
    steps = [(0, 1), (1, -1)]
    sides = lax.ppermute(
        weight,
        ("core", "rep"),
        [(c * reps + (i + k) % reps, c * reps + i) for c, k in steps for i in range(reps)],
    )
    across = lax.ppermute(weight, "rep", [((i + 2) % reps, i) for i in range(reps)])
    sides = lax.all_gather(sides, "core", axis=0)
    return [sides[0], across, sides[1]]


def swap_cores(x):
    return lax.ppermute(x, "core", [(0, 1), (1, 0)])


def exchange(x, axis):
    return lax.all_to_all(x, axis, 0, 0, tiled=True)


def body(tile_values, tile_rows, tile_cols, tile_count, features, weight, cotangent):
    values = tile_values[0, 0]
    core = lax.axis_index("core").astype(jnp.int32).reshape(1)
    rep = lax.axis_index("rep").astype(jnp.int32).reshape(1)
    side = values.shape[-1]
    width = features.shape[1]
    grains, total = cotangent.shape
    ys, rows, reps = (lax.axis_size(a) for a in ("y", "row", "rep"))
    col_blocks = features.shape[0] // side
    row_blocks = 2 * ys * grains // side
    nodes = grains * rows * ys * 2
    holders = min(HOLDERS, ys)

    ids = pack_ids(tile_rows[0, 0], tile_cols[0, 0], tile_count[0, 0], row_blocks, col_blocks)
    feats = features.reshape(col_blocks, side, width)
    own, other = forward_tiles(core, ids, values, feats, ys, grains)
    pair, lent = add_pair(own, swap_cores(other), weight)
    parts = exchange(pair, "y")
    others = fetch_others(lent)
    aggs = exchange(fold(parts, reps, others), "rep")
    activation, payload = dense(rep, aggs, [weight, *others], cotangent, ys, side)
    mine = exchange(payload, "y")
    theirs = swap_cores(mine)
    back = backward_tiles(ids, core, values, mine, theirs, rows, col_blocks)
    sums = exchange(back, "row")
    grad, share = finish(sums, 1.0 / math.sqrt(nodes), grains, width // holders, total)
    input_grad = exchange(grad, "row")
    groups = [list(range(y, y + holders)) for y in range(0, ys, holders)]
    weight_grad = lax.all_gather(share, "y", axis_index_groups=groups, tiled=True)
    return (activation, weight_grad, input_grad)


def solution(mesh):
    rows, cols, reps = mesh.devices.shape
    split = Mesh(
        mesh.devices.reshape(rows, cols // 2, 2, reps), ("row", "y", "core", "rep")
    )
    col = ("y", "core")
    return jax.shard_map(
        body,
        mesh=split,
        in_specs=(
            P("row", col, None, None, None),
            P("row", col, None),
            P("row", col, None),
            P("row", col),
            P(col, "rep"),
            P("rep", None),
            P(("row",) + col, None),
        ),
        out_specs=(P(("row",) + col, None), P("rep", None), P(col, "rep")),
        check_vma=False,
    )
```

```python
import functools
import math

import jax
import jax.numpy as jnp
from jax import lax
from jax.experimental import pallas as pl
from jax.experimental.pallas import tpu as pltpu
from jax.sharding import Mesh
from jax.sharding import PartitionSpec as P

VMEM_LIMIT = 40 * 1024 * 1024
FORWARD_VMEM = 51 * 1024 * 1024
CHUNK = 16
BF = jnp.bfloat16
F4 = jnp.float32

VMEM = pl.BlockSpec(memory_space=pltpu.VMEM)
SMEM = pl.BlockSpec(memory_space=pltpu.SMEM)
ANY = pl.BlockSpec(memory_space=pl.ANY)
HOLDERS = 4


def dot(a, b, dims=(((1,), (0,)), ((), ()))):
    return lax.dot_general(a, b, dims, preferred_element_type=F4)


def tile_copies(values, tiles, sems):
    return [
        pltpu.make_async_copy(
            values.at[pl.ds(first, CHUNK)], tiles.at[pl.ds(first, CHUNK)], sems.at[first // CHUNK]
        )
        for first in range(0, tiles.shape[0], CHUNK)
    ]


def pack_ids(row_ids, col_ids, used, row_blocks, col_blocks, *extra):
    slots = row_ids.shape[0]
    at = jnp.arange(slots + len(extra), dtype=jnp.int32)
    span = 2 * col_blocks
    words = jnp.pad(row_ids * span + col_ids, (0, len(extra)))
    words = jnp.where(at < used, words, row_blocks * span + col_blocks)
    for k, word in enumerate(extra):
        words = jnp.where(at == slots + k, word, words)
    return words


def forward_kernel(ids_any, values, feats_any, own, other, ids, feats, tiles, acc, sems, more_sems):
    first = [
        pltpu.make_async_copy(ids_any, ids, more_sems.at[0]),
        pltpu.make_async_copy(feats_any, feats, more_sems.at[1]),
    ]
    copies = tile_copies(values, tiles, sems)
    for copy in first + copies:
        copy.start()
    acc[...] = jnp.zeros_like(acc)
    for copy in first:
        copy.wait()
    slots = tiles.shape[0]
    col_blocks, side, _ = feats.shape
    row_shift = col_blocks.bit_length()
    for chunk, copy in enumerate(copies):
        copy.wait()
        for t in range(chunk * CHUNK, (chunk + 1) * CHUNK):
            acc[ids[t] >> row_shift] += dot(tiles[t], feats[ids[t] & (col_blocks - 1)])
    ys, grains, _ = own.shape
    blocks = grains // side
    me = ids[slots]
    for y in range(ys):
        for b in range(blocks):
            rows = pl.ds(b * side, side)
            own[y, rows, :] = acc[(2 * y + me) * blocks + b]
            other[y, rows, :] = acc[(2 * y + 1 - me) * blocks + b].astype(BF)


def forward_tiles(ids, values, feats, ys, grains):
    slots, side, _ = values.shape
    width = feats.shape[-1]
    row_blocks = 2 * ys * grains // side
    return pl.pallas_call(
        forward_kernel,
        out_shape=(
            jax.ShapeDtypeStruct((ys, grains, width), F4),
            jax.ShapeDtypeStruct((ys, grains, width), BF),
        ),
        in_specs=[ANY, ANY, ANY],
        out_specs=(VMEM, VMEM),
        scratch_shapes=[
            pltpu.SMEM(ids.shape, jnp.int32),
            pltpu.VMEM(feats.shape, BF),
            pltpu.VMEM((slots, side, side), BF),
            pltpu.VMEM((row_blocks + 1, side, width), F4),
            pltpu.SemaphoreType.DMA((slots // CHUNK,)),
            pltpu.SemaphoreType.DMA((2,)),
        ],
        compiler_params=pltpu.CompilerParams(vmem_limit_bytes=FORWARD_VMEM),
        name="forward_tiles",
    )(ids, values, feats)


def fold_kernel(parts, *refs):
    copies = refs[-1]
    total = parts[0].astype(F4)
    for y in range(1, parts.shape[0]):
        total += parts[y].astype(F4)
    total = total.astype(BF)
    for q in range(copies.shape[0]):
        copies[q] = total


def fold(parts, copies, before):
    return pl.pallas_call(
        fold_kernel,
        out_shape=jax.ShapeDtypeStruct((copies,) + parts.shape[1:], BF),
        in_specs=[VMEM] + [ANY] * len(before),
        out_specs=VMEM,
        compiler_params=pltpu.CompilerParams(vmem_limit_bytes=VMEM_LIMIT),
        name="fold",
    )(parts, *before)


def dense_kernel(rep_at, ids, aggs, own_weight, *refs):
    reps, grains, width = aggs.shape
    others, (cot, act, payload) = refs[: reps - 1], refs[reps - 1 :]
    me = ids[rep_at]
    ys, _, side = payload.shape
    own_agg = aggs[me]
    hidden = dot(own_agg, own_weight[...])
    for k, weight in enumerate(others):
        hidden += dot(aggs[(me + k + 1) % reps], weight[...])
    sigma = jax.nn.sigmoid(hidden)
    act[...] = (hidden * sigma).astype(BF)
    slope = sigma * (1.0 + hidden * (1.0 - sigma))
    grad_hidden = (cot[...].astype(F4) * slope).astype(BF)
    back = dot(own_weight[...], grad_hidden, (((1,), (1,)), ((), ()))).astype(BF)
    share = dot(own_agg, grad_hidden, (((0,), (0,)), ((), ()))).astype(BF)
    holders = min(HOLDERS, ys)
    part = width // holders
    base = grains // side * width
    for y in range(ys):
        for b in range(grains // side):
            payload[y, pl.ds(b * width, width), :] = back[:, b * side : (b + 1) * side]
        chunk = y % holders
        for k in range(share.shape[1] // side):
            payload[y, pl.ds(base + k * part, part), :] = share[
                chunk * part : (chunk + 1) * part, k * side : (k + 1) * side
            ]


def dense(ids, aggs, weights, cot, ys, side):
    reps, grains, width = aggs.shape
    total = cot.shape[1]
    rows = grains // side * width + width // min(HOLDERS, ys) * (total // side)
    return pl.pallas_call(
        functools.partial(dense_kernel, ids.shape[0] - 1),
        out_shape=(
            jax.ShapeDtypeStruct((grains, total), BF),
            jax.ShapeDtypeStruct((ys, rows, side), BF),
        ),
        in_specs=[SMEM] + [VMEM] * (reps + 2),
        out_specs=(VMEM, VMEM),
        compiler_params=pltpu.CompilerParams(vmem_limit_bytes=VMEM_LIMIT),
        name="dense",
    )(ids, aggs, *weights, cot)


def backward_kernel(ids, tiles, mine, theirs, payload, acc):
    acc[...] = jnp.zeros_like(acc)
    side = tiles.shape[1]
    width = acc.shape[1]
    rows = payload.shape[0]
    ys = mine.shape[0]
    col_blocks = acc.shape[0] - 1
    per_row = col_blocks // rows
    base = per_row * width

    slots = tiles.shape[0]
    row_shift = col_blocks.bit_length()
    core_shift = row_shift + per_row.bit_length() - 1
    me = ids[slots]
    for t in range(slots):
        word = ids[t]
        start = ((word >> row_shift) & (per_row - 1)) * width
        block = pl.ds(pl.multiple_of(start, width), width)
        y = (word >> (core_shift + 1)) & (ys - 1)
        local = ((word >> core_shift) & 1) == me
        grad = jnp.where(local, mine[y, block], theirs[y, block])
        acc[word & (2 * col_blocks - 1)] += dot(grad, tiles[t])
    share = jnp.zeros((payload.shape[1] - base, side), F4)
    for grads in (mine, theirs):
        for y in range(ys):
            share += grads[y, base:, :].astype(F4)
    share = share.astype(BF)
    for r in range(rows):
        for b in range(per_row):
            payload[r, pl.ds(b * width, width), :] = acc[r * per_row + b].astype(BF)
        payload[r, base:, :] = share


def backward_tiles(ids, values, mine, theirs, rows, col_blocks):
    side = values.shape[1]
    length = mine.shape[1]
    return pl.pallas_call(
        backward_kernel,
        out_shape=jax.ShapeDtypeStruct((rows, length, side), BF),
        in_specs=[SMEM] + [VMEM] * 3,
        out_specs=VMEM,
        scratch_shapes=[pltpu.VMEM((col_blocks + 1, side, side), F4)],
        compiler_params=pltpu.CompilerParams(vmem_limit_bytes=VMEM_LIMIT),
        name="backward_tiles",
    )(ids, values, mine, theirs)


def finish_kernel(scale, parts, grad, share):
    rows, length, side = parts.shape
    width = side
    grains = grad.shape[0] // rows
    base = grains // side * width
    total = parts[0].astype(F4)
    for r in range(1, rows):
        total += parts[r].astype(F4)
    for b in range(grains // side):
        block = total[b * width : (b + 1) * width].T.astype(BF)
        for r in range(rows):
            grad[pl.ds(r * grains + b * side, side), :] = block
    part = share.shape[0]
    for k in range(share.shape[1] // side):
        share[:, k * side : (k + 1) * side] = total[base + k * part : base + (k + 1) * part] * scale


def finish(parts, scale, grains, part, total):
    rows, length, side = parts.shape
    return pl.pallas_call(
        functools.partial(finish_kernel, scale),
        out_shape=(
            jax.ShapeDtypeStruct((rows * grains, side), BF),
            jax.ShapeDtypeStruct((part, total), F4),
        ),
        in_specs=[VMEM],
        out_specs=(VMEM, VMEM),
        compiler_params=pltpu.CompilerParams(vmem_limit_bytes=VMEM_LIMIT),
        name="finish",
    )(parts)


def deliver_kernel(holders, chunk_at, ids, grad, *refs):
    pieces, (grad_out, weight_out, sems) = refs[:holders], refs[holders:]
    part = weight_out.shape[0] // holders
    copies = [pltpu.make_async_copy(grad, grad_out, sems.at[holders])]
    for k, piece in enumerate(pieces):
        start = ((ids[chunk_at] + k) & (holders - 1)) * part
        place = weight_out.at[pl.ds(pl.multiple_of(start, part), part)]
        copies.append(pltpu.make_async_copy(piece, place, sems.at[k]))
    for copy in copies:
        copy.start()
    for copy in copies:
        copy.wait()


def deliver(ids, chunk_at, grad, pieces):
    holders = len(pieces)
    part, total = pieces[0].shape
    return pl.pallas_call(
        functools.partial(deliver_kernel, holders, chunk_at),
        out_shape=(
            jax.ShapeDtypeStruct(grad.shape, BF),
            jax.ShapeDtypeStruct((part * holders, total), F4),
        ),
        in_specs=[SMEM] + [ANY] * (1 + holders),
        out_specs=(ANY, ANY),
        scratch_shapes=[pltpu.SemaphoreType.DMA((holders + 1,))],
        compiler_params=pltpu.CompilerParams(vmem_limit_bytes=VMEM_LIMIT),
        name="deliver",
    )(ids, grad, *pieces)


def around(x, axis, count):
    n = lax.axis_size(axis)
    if count != 4:
        return [
            lax.ppermute(x, axis, [((i + k) % n, i) for i in range(n)]) for k in range(1, count)
        ]
    names, place = (("y", "core"), (2, 1)) if axis == "y" else (("core", axis), (1, n))
    step, core = place
    sides = lax.ppermute(
        x,
        names,
        [
            ((i + k) % n * step + c * core, i * step + c * core)
            for c, k in ((0, 1), (1, -1))
            for i in range(n)
        ],
    )
    across = lax.ppermute(x, axis, [((i + 2) % n, i) for i in range(n)])
    sides = lax.all_gather(sides, "core", axis=0)
    return [sides[0], across, sides[1]]


def swap_cores(x):
    return lax.ppermute(x, "core", [(0, 1), (1, 0)])


def exchange(x, axis):
    return lax.all_to_all(x, axis, 0, 0, tiled=True)


def body(tile_values, tile_rows, tile_cols, tile_count, features, weight, cotangent):
    values = tile_values[0, 0]
    side = values.shape[-1]
    width = features.shape[1]
    grains, total = cotangent.shape
    ys, rows, reps = (lax.axis_size(a) for a in ("y", "row", "rep"))
    col_blocks = features.shape[0] // side
    row_blocks = 2 * ys * grains // side
    nodes = grains * rows * ys * 2
    holders = min(HOLDERS, ys)

    slots = values.shape[0]
    where = [lax.axis_index(a).astype(jnp.int32) for a in ("core", "y", "rep")]
    ids = pack_ids(
        tile_rows[0, 0], tile_cols[0, 0], tile_count[0, 0], row_blocks, col_blocks, *where
    )
    feats = features.reshape(col_blocks, side, width)
    own, other = forward_tiles(ids, values, feats, ys, grains)
    pair = (own + swap_cores(other).astype(F4)).astype(BF)
    pair, lent = lax.optimization_barrier((pair, weight))
    parts = exchange(pair, "y")
    others = around(lent, "rep", reps)
    aggs = exchange(fold(parts, reps, others), "rep")
    activation, payload = dense(ids, aggs, [weight, *others], cotangent, ys, side)
    mine = exchange(payload, "y")
    theirs = swap_cores(mine)
    back = backward_tiles(ids, values, mine, theirs, rows, col_blocks)
    sums = exchange(back, "row")
    grad, share = finish(sums, 1.0 / math.sqrt(nodes), grains, width // holders, total)
    input_grad = exchange(grad, "row")
    input_grad, weight_grad = deliver(
        ids, slots + 1, input_grad, [share, *around(share, "y", holders)]
    )
    return (activation, weight_grad, input_grad)


def solution(mesh):
    rows, cols, reps = mesh.devices.shape
    split = Mesh(
        mesh.devices.reshape(rows, cols // 2, 2, reps), ("row", "y", "core", "rep")
    )
    col = ("y", "core")
    return jax.shard_map(
        body,
        mesh=split,
        in_specs=(
            P("row", col, None, None, None),
            P("row", col, None),
            P("row", col, None),
            P("row", col),
            P(col, "rep"),
            P("rep", None),
            P(("row",) + col, None),
        ),
        out_specs=(P(("row",) + col, None), P("rep", None), P(col, "rep")),
        check_vma=False,
    )
```

```python
import functools
import math

import jax
import jax.numpy as jnp
from jax import lax
from jax.experimental import pallas as pl
from jax.experimental.pallas import tpu as pltpu
from jax.sharding import Mesh
from jax.sharding import PartitionSpec as P

VMEM_LIMIT = 40 * 1024 * 1024
PIECES = 2
BF = jnp.bfloat16
F4 = jnp.float32

VMEM = pl.BlockSpec(memory_space=pltpu.VMEM)
SMEM = pl.BlockSpec(memory_space=pltpu.SMEM)
ANY = pl.BlockSpec(memory_space=pl.ANY)
HOLDERS = 4


def in_hbm(x):
    return pltpu.with_memory_space_constraint(x, pltpu.HBM)


def dot(a, b, dims=(((1,), (0,)), ((), ()))):
    return lax.dot_general(a, b, dims, preferred_element_type=F4)


def tile_copies(values, tiles, sems):
    piece = tiles.shape[0] // PIECES
    spans = [pl.ds(k * piece, piece) for k in range(PIECES)]
    return [
        pltpu.make_async_copy(values.at[span], tiles.at[span], sems.at[k])
        for k, span in enumerate(spans)
    ]


def pack_ids(row_ids, col_ids, used, row_blocks, col_blocks, *extra):
    slots = row_ids.shape[0]
    at = jnp.arange(slots, dtype=jnp.int32)
    span = 2 * col_blocks
    words = jnp.where(at < used, row_ids * span + col_ids, row_blocks * span + col_blocks)
    at = jnp.arange(slots + len(extra), dtype=jnp.int32)
    words = jnp.pad(words, (0, len(extra)))
    for k, word in enumerate(extra):
        words = jnp.where(at == slots + k, word, words)
    return words


def forward_kernel(ids_any, values, feats_any, own, other, ids, feats, tiles, acc, sems, more_sems):
    first = [
        pltpu.make_async_copy(ids_any, ids, more_sems.at[0]),
        pltpu.make_async_copy(feats_any, feats, more_sems.at[1]),
    ]
    copies = tile_copies(values, tiles, sems)
    for copy in first + copies:
        copy.start()
    acc[...] = jnp.zeros_like(acc)
    for copy in first:
        copy.wait()
    slots = tiles.shape[0]
    col_blocks, side, _ = feats.shape
    row_shift = col_blocks.bit_length()
    piece = slots // PIECES
    for k, copy in enumerate(copies):
        copy.wait()
        for t in range(k * piece, (k + 1) * piece):
            acc[ids[t] >> row_shift] += dot(tiles[t], feats[ids[t] & (col_blocks - 1)])
    ys, grains, _ = own.shape
    blocks = grains // side
    me = ids[slots]
    for y in range(ys):
        for b in range(blocks):
            rows = pl.ds(b * side, side)
            own[y, rows, :] = acc[(2 * y + me) * blocks + b]
            other[y, rows, :] = acc[(2 * y + 1 - me) * blocks + b].astype(BF)


def forward_tiles(ids, values, feats, ys, grains):
    slots, side, _ = values.shape
    width = feats.shape[-1]
    row_blocks = 2 * ys * grains // side
    return pl.pallas_call(
        forward_kernel,
        out_shape=(
            jax.ShapeDtypeStruct((ys, grains, width), F4),
            jax.ShapeDtypeStruct((ys, grains, width), BF),
        ),
        in_specs=[ANY, ANY, ANY],
        out_specs=(VMEM, VMEM),
        scratch_shapes=[
            pltpu.SMEM(ids.shape, jnp.int32),
            pltpu.VMEM(feats.shape, BF),
            pltpu.VMEM((slots, side, side), BF),
            pltpu.VMEM((row_blocks + 1, side, width), F4),
            pltpu.SemaphoreType.DMA((PIECES,)),
            pltpu.SemaphoreType.DMA((2,)),
        ],
        compiler_params=pltpu.CompilerParams(vmem_limit_bytes=VMEM_LIMIT),
        name="forward_tiles",
    )(ids, in_hbm(values), in_hbm(feats))


def fold_kernel(parts_hbm, weight_hbm, cot_hbm, *refs):
    copies, weight, cot, parts, sems, more_sems = refs[-6:]
    bring = [
        pltpu.make_async_copy(parts_hbm.at[y], parts.at[y], sems.at[y])
        for y in range(parts.shape[0])
    ]
    more = [
        pltpu.make_async_copy(weight_hbm, weight, more_sems.at[0]),
        pltpu.make_async_copy(cot_hbm, cot, more_sems.at[1]),
    ]
    for copy in bring + more:
        copy.start()
    bring[0].wait()
    total = parts[0].astype(F4)
    for y in range(1, parts.shape[0]):
        bring[y].wait()
        total += parts[y].astype(F4)
    total = total.astype(BF)
    for q in range(copies.shape[0]):
        copies[q] = total
    for copy in more:
        copy.wait()


def fold(parts, weight, cot, copies, before):
    return pl.pallas_call(
        fold_kernel,
        out_shape=(
            jax.ShapeDtypeStruct((copies,) + parts.shape[1:], BF),
            pltpu.VMEM(weight.shape, BF),
            pltpu.VMEM(cot.shape, BF),
        ),
        in_specs=[ANY] * (3 + len(before)),
        out_specs=(VMEM,) * 3,
        scratch_shapes=[
            pltpu.VMEM(parts.shape, BF),
            pltpu.SemaphoreType.DMA(parts.shape[:1]),
            pltpu.SemaphoreType.DMA((2,)),
        ],
        compiler_params=pltpu.CompilerParams(vmem_limit_bytes=VMEM_LIMIT),
        name="fold",
    )(in_hbm(parts), in_hbm(weight), in_hbm(cot), *before)


def dense_kernel(rep_at, ids, aggs, own_weight, *refs):
    reps, grains, width = aggs.shape
    others, (cot, act_hbm, payload, act, sem) = refs[: reps - 1], refs[reps - 1 :]
    take_act = pltpu.make_async_copy(act, act_hbm, sem)
    me = ids[rep_at]
    ys, _, side = payload.shape
    own_agg = aggs[me]
    hidden = dot(own_agg, own_weight[...])
    for k, weight in enumerate(others):
        hidden += dot(aggs[(me + k + 1) % reps], weight[...])
    sigma = jax.nn.sigmoid(hidden)
    act[...] = (hidden * sigma).astype(BF)
    take_act.start()
    slope = sigma * (1.0 + hidden * (1.0 - sigma))
    grad_hidden = (cot[...].astype(F4) * slope).astype(BF)
    back = dot(own_weight[...], grad_hidden, (((1,), (1,)), ((), ()))).astype(BF)
    share = dot(own_agg, grad_hidden, (((0,), (0,)), ((), ()))).astype(BF)
    holders = min(HOLDERS, ys)
    part = width // holders
    base = grains // side * width
    for y in range(ys):
        for b in range(grains // side):
            payload[y, pl.ds(b * width, width), :] = back[:, b * side : (b + 1) * side]
        chunk = y % holders
        for k in range(share.shape[1] // side):
            payload[y, pl.ds(base + k * part, part), :] = share[
                chunk * part : (chunk + 1) * part, k * side : (k + 1) * side
            ]
    take_act.wait()


def dense(ids, aggs, weight, others, cot, ys, side):
    reps, grains, width = aggs.shape
    total = cot.shape[1]
    rows = grains // side * width + width // min(HOLDERS, ys) * (total // side)
    return pl.pallas_call(
        functools.partial(dense_kernel, ids.shape[0] - 1),
        out_shape=(
            jax.ShapeDtypeStruct((grains, total), BF),
            jax.ShapeDtypeStruct((ys, rows, side), BF),
        ),
        in_specs=[SMEM] + [VMEM] * (2 + reps),
        out_specs=(ANY, VMEM),
        scratch_shapes=[pltpu.VMEM((grains, total), BF), pltpu.SemaphoreType.DMA],
        compiler_params=pltpu.CompilerParams(vmem_limit_bytes=VMEM_LIMIT),
        name="dense",
    )(ids, aggs, weight, *others, cot)


def backward_kernel(ids, tiles, mine, theirs, payload, acc):
    acc[...] = jnp.zeros_like(acc)
    side = tiles.shape[1]
    width = acc.shape[1]
    rows = payload.shape[0]
    ys = mine.shape[0]
    col_blocks = acc.shape[0] - 1
    per_row = col_blocks // rows
    base = per_row * width

    slots = tiles.shape[0]
    row_shift = col_blocks.bit_length()
    core_shift = row_shift + per_row.bit_length() - 1
    me = ids[slots]
    for t in range(slots):
        word = ids[t]
        start = ((word >> row_shift) & (per_row - 1)) * width
        block = pl.ds(pl.multiple_of(start, width), width)
        y = (word >> (core_shift + 1)) & (ys - 1)
        local = ((word >> core_shift) & 1) == me
        grad = jnp.where(local, mine[y, block], theirs[y, block])
        acc[word & (2 * col_blocks - 1)] += dot(grad, tiles[t])
    share = jnp.zeros((payload.shape[1] - base, side), F4)
    for grads in (mine, theirs):
        for y in range(ys):
            share += grads[y, base:, :].astype(F4)
    share = share.astype(BF)
    for r in range(rows):
        for b in range(per_row):
            payload[r, pl.ds(b * width, width), :] = acc[r * per_row + b].astype(BF)
        payload[r, base:, :] = share


def backward_tiles(ids, values, mine, theirs, rows, col_blocks):
    side = values.shape[1]
    length = mine.shape[1]
    return pl.pallas_call(
        backward_kernel,
        out_shape=jax.ShapeDtypeStruct((rows, length, side), BF),
        in_specs=[SMEM] + [VMEM] * 3,
        out_specs=VMEM,
        scratch_shapes=[pltpu.VMEM((col_blocks + 1, side, side), F4)],
        compiler_params=pltpu.CompilerParams(vmem_limit_bytes=VMEM_LIMIT),
        name="backward_tiles",
    )(ids, values, mine, theirs)


def finish_kernel(scale, parts, grad, share):
    rows, length, side = parts.shape
    width = side
    grains = grad.shape[0] // rows
    base = grains // side * width
    total = parts[0].astype(F4)
    for r in range(1, rows):
        total += parts[r].astype(F4)
    for b in range(grains // side):
        block = total[b * width : (b + 1) * width].T.astype(BF)
        for r in range(rows):
            grad[pl.ds(r * grains + b * side, side), :] = block
    part = share.shape[0]
    for k in range(share.shape[1] // side):
        share[:, k * side : (k + 1) * side] = total[base + k * part : base + (k + 1) * part] * scale


def finish(parts, scale, grains, part, total):
    rows, length, side = parts.shape
    return pl.pallas_call(
        functools.partial(finish_kernel, scale),
        out_shape=(
            jax.ShapeDtypeStruct((rows * grains, side), BF),
            jax.ShapeDtypeStruct((part, total), F4),
        ),
        in_specs=[VMEM],
        out_specs=(VMEM, VMEM),
        compiler_params=pltpu.CompilerParams(vmem_limit_bytes=VMEM_LIMIT),
        name="finish",
    )(parts)


def place_kernel(chunk_at, ids, *refs):
    pieces, out = refs[:-1], refs[-1]
    part = pieces[0].shape[0]
    for k, piece in enumerate(pieces):
        start = ((ids[chunk_at] + k) & (len(pieces) - 1)) * part
        out[pl.ds(pl.multiple_of(start, part), part), :] = piece[...]


def place(ids, chunk_at, pieces):
    part, total = pieces[0].shape
    return pl.pallas_call(
        functools.partial(place_kernel, chunk_at),
        out_shape=jax.ShapeDtypeStruct((part * len(pieces), total), F4),
        in_specs=[SMEM] + [VMEM] * len(pieces),
        out_specs=VMEM,
        compiler_params=pltpu.CompilerParams(vmem_limit_bytes=VMEM_LIMIT),
        name="place",
    )(ids, *pieces)


def around(x, axis, count):
    n = lax.axis_size(axis)
    if count != 4:
        return [
            lax.ppermute(x, axis, [((i + k) % n, i) for i in range(n)]) for k in range(1, count)
        ]
    names, place = (("y", "core"), (2, 1)) if axis == "y" else (("core", axis), (1, n))
    step, core = place
    sides = lax.ppermute(
        x,
        names,
        [
            ((i + k) % n * step + c * core, i * step + c * core)
            for c, k in ((0, 1), (1, -1))
            for i in range(n)
        ],
    )
    across = lax.ppermute(x, axis, [((i + 2) % n, i) for i in range(n)])
    sides = lax.all_gather(sides, "core", axis=0)
    return [sides[0], across, sides[1]]


def swap_cores(x):
    return lax.ppermute(x, "core", [(0, 1), (1, 0)])


def exchange(x, axis):
    return lax.all_to_all(x, axis, 0, 0, tiled=True)


def body(tile_values, tile_rows, tile_cols, tile_count, features, weight, cotangent):
    values = tile_values[0, 0]
    side = values.shape[-1]
    width = features.shape[1]
    grains, total = cotangent.shape
    ys, rows, reps = (lax.axis_size(a) for a in ("y", "row", "rep"))
    col_blocks = features.shape[0] // side
    row_blocks = 2 * ys * grains // side
    nodes = grains * rows * ys * 2
    holders = min(HOLDERS, ys)

    slots = values.shape[0]
    where = [lax.axis_index(a).astype(jnp.int32) for a in ("core", "y", "rep")]
    ids = pack_ids(
        tile_rows[0, 0], tile_cols[0, 0], tile_count[0, 0], row_blocks, col_blocks, *where
    )
    feats = features.reshape(col_blocks, side, width)
    own, other = forward_tiles(ids, values, feats, ys, grains)
    pair = (own + swap_cores(other).astype(F4)).astype(BF)
    pair, lent = lax.optimization_barrier((pair, weight))
    parts = exchange(pair, "y")
    others = around(lent, "rep", reps)
    copies, near, cot = fold(parts, weight, cotangent, reps, others)
    aggs = exchange(copies, "rep")
    activation, payload = dense(ids, aggs, near, others, cot, ys, side)
    mine = exchange(payload, "y")
    theirs = swap_cores(mine)
    back = backward_tiles(ids, values, mine, theirs, rows, col_blocks)
    sums = exchange(back, "row")
    grad, share = finish(sums, 1.0 / math.sqrt(nodes), grains, width // holders, total)
    input_grad = exchange(grad, "row")
    weight_grad = place(ids, slots + 1, [share, *around(share, "y", holders)])
    return (activation, weight_grad, input_grad)


def solution(mesh):
    rows, cols, reps = mesh.devices.shape
    split = Mesh(
        mesh.devices.reshape(rows, cols // 2, 2, reps), ("row", "y", "core", "rep")
    )
    col = ("y", "core")
    return jax.shard_map(
        body,
        mesh=split,
        in_specs=(
            P("row", col, None, None, None),
            P("row", col, None),
            P("row", col, None),
            P("row", col),
            P(col, "rep"),
            P("rep", None),
            P(("row",) + col, None),
        ),
        out_specs=(P(("row",) + col, None), P("rep", None), P(col, "rep")),
        check_vma=False,
    )
```

```python
import functools
import math

import jax
import jax.numpy as jnp
from jax import lax
from jax.experimental import pallas as pl
from jax.experimental.pallas import tpu as pltpu
from jax.sharding import Mesh
from jax.sharding import PartitionSpec as P

VMEM_LIMIT = 40 * 1024 * 1024
PIECES = 2
BF = jnp.bfloat16
F4 = jnp.float32

VMEM = pl.BlockSpec(memory_space=pltpu.VMEM)
SMEM = pl.BlockSpec(memory_space=pltpu.SMEM)
ANY = pl.BlockSpec(memory_space=pl.ANY)
HOLDERS = 4


def in_hbm(x):
    return pltpu.with_memory_space_constraint(x, pltpu.HBM)


def dot(a, b, dims=(((1,), (0,)), ((), ()))):
    return lax.dot_general(a, b, dims, preferred_element_type=F4)


def tile_copies(values, tiles, sems):
    piece = tiles.shape[0] // PIECES
    spans = [pl.ds(k * piece, piece) for k in range(PIECES)]
    return [
        pltpu.make_async_copy(values.at[span], tiles.at[span], sems.at[k])
        for k, span in enumerate(spans)
    ]


def pack_ids(row_ids, col_ids, used, row_blocks, col_blocks, *extra):
    slots = row_ids.shape[0]
    at = jnp.arange(slots, dtype=jnp.int32)
    span = 2 * col_blocks
    words = jnp.where(at < used, row_ids * span + col_ids, row_blocks * span + col_blocks)
    at = jnp.arange(slots + len(extra), dtype=jnp.int32)
    words = jnp.pad(words, (0, len(extra)))
    for k, word in enumerate(extra):
        words = jnp.where(at == slots + k, word, words)
    return words


def forward_kernel(ids_any, values, feats_any, own, other, ids, feats, tiles, acc, sems, more_sems):
    first = [
        pltpu.make_async_copy(ids_any, ids, more_sems.at[0]),
        pltpu.make_async_copy(feats_any, feats, more_sems.at[1]),
    ]
    copies = tile_copies(values, tiles, sems)
    for copy in first + copies:
        copy.start()
    acc[...] = jnp.zeros_like(acc)
    for copy in first:
        copy.wait()
    slots = tiles.shape[0]
    col_blocks, side, _ = feats.shape
    row_shift = col_blocks.bit_length()
    piece = slots // PIECES
    for k, copy in enumerate(copies):
        copy.wait()
        for t in range(k * piece, (k + 1) * piece):
            acc[ids[t] >> row_shift] += dot(tiles[t], feats[ids[t] & (col_blocks - 1)])
    ys, grains, _ = own.shape
    blocks = grains // side
    me = ids[slots]
    for y in range(ys):
        for b in range(blocks):
            rows = pl.ds(b * side, side)
            own[y, rows, :] = acc[(2 * y + me) * blocks + b]
            other[y, rows, :] = acc[(2 * y + 1 - me) * blocks + b].astype(BF)


def forward_tiles(ids, values, feats, ys, grains):
    slots, side, _ = values.shape
    width = feats.shape[-1]
    row_blocks = 2 * ys * grains // side
    return pl.pallas_call(
        forward_kernel,
        out_shape=(
            jax.ShapeDtypeStruct((ys, grains, width), F4),
            jax.ShapeDtypeStruct((ys, grains, width), BF),
        ),
        in_specs=[ANY, ANY, ANY],
        out_specs=(VMEM, VMEM),
        scratch_shapes=[
            pltpu.SMEM(ids.shape, jnp.int32),
            pltpu.VMEM(feats.shape, BF),
            pltpu.VMEM((slots, side, side), BF),
            pltpu.VMEM((row_blocks + 1, side, width), F4),
            pltpu.SemaphoreType.DMA((PIECES,)),
            pltpu.SemaphoreType.DMA((2,)),
        ],
        compiler_params=pltpu.CompilerParams(vmem_limit_bytes=VMEM_LIMIT),
        name="forward_tiles",
    )(ids, in_hbm(values), in_hbm(feats))


def fold_kernel(parts_hbm, weight_hbm, cot_hbm, *refs):
    copies, weight, cot, parts, sems, more_sems = refs[-6:]
    bring = [
        pltpu.make_async_copy(parts_hbm.at[y], parts.at[y], sems.at[y])
        for y in range(parts.shape[0])
    ]
    more = [
        pltpu.make_async_copy(weight_hbm, weight, more_sems.at[0]),
        pltpu.make_async_copy(cot_hbm, cot, more_sems.at[1]),
    ]
    for copy in bring + more:
        copy.start()
    bring[0].wait()
    total = parts[0].astype(F4)
    for y in range(1, parts.shape[0]):
        bring[y].wait()
        total += parts[y].astype(F4)
    total = total.astype(BF)
    for q in range(copies.shape[0]):
        copies[q] = total
    for copy in more:
        copy.wait()


def fold(parts, weight, cot, copies, before):
    return pl.pallas_call(
        fold_kernel,
        out_shape=(
            jax.ShapeDtypeStruct((copies,) + parts.shape[1:], BF),
            pltpu.VMEM(weight.shape, BF),
            pltpu.VMEM(cot.shape, BF),
        ),
        in_specs=[ANY] * (3 + len(before)),
        out_specs=(VMEM,) * 3,
        scratch_shapes=[
            pltpu.VMEM(parts.shape, BF),
            pltpu.SemaphoreType.DMA(parts.shape[:1]),
            pltpu.SemaphoreType.DMA((2,)),
        ],
        compiler_params=pltpu.CompilerParams(vmem_limit_bytes=VMEM_LIMIT),
        name="fold",
    )(in_hbm(parts), in_hbm(weight), in_hbm(cot), *before)


def dense_kernel(rep_at, ids, aggs, own_weight, *refs):
    reps, grains, width = aggs.shape
    others, (cot, act_hbm, payload, act, sem) = refs[: reps - 1], refs[reps - 1 :]
    take_act = pltpu.make_async_copy(act, act_hbm, sem)
    me = ids[rep_at]
    ys, _, side = payload.shape
    own_agg = aggs[me]
    hidden = dot(own_agg, own_weight[...])
    for k, weight in enumerate(others):
        hidden += dot(aggs[(me + k + 1) % reps], weight[...])
    sigma = jax.nn.sigmoid(hidden)
    act[...] = (hidden * sigma).astype(BF)
    take_act.start()
    slope = sigma * (1.0 + hidden * (1.0 - sigma))
    grad_hidden = (cot[...].astype(F4) * slope).astype(BF)
    back = dot(own_weight[...], grad_hidden, (((1,), (1,)), ((), ()))).astype(BF)
    share = dot(own_agg, grad_hidden, (((0,), (0,)), ((), ()))).astype(BF)
    holders = min(HOLDERS, ys)
    part = width // holders
    base = grains // side * width
    for y in range(ys):
        for b in range(grains // side):
            payload[y, pl.ds(b * width, width), :] = back[:, b * side : (b + 1) * side]
        for k in range(share.shape[1] // side):
            for c in range(2):
                rows = c * (width // 2) + y % holders * (part // 2)
                payload[y, pl.ds(base + k * part + c * (part // 2), part // 2), :] = share[
                    rows : rows + part // 2, k * side : (k + 1) * side
                ]
    take_act.wait()


def dense(ids, aggs, weight, others, cot, ys, side):
    reps, grains, width = aggs.shape
    total = cot.shape[1]
    rows = grains // side * width + width // min(HOLDERS, ys) * (total // side)
    return pl.pallas_call(
        functools.partial(dense_kernel, ids.shape[0] - 1),
        out_shape=(
            jax.ShapeDtypeStruct((grains, total), BF),
            jax.ShapeDtypeStruct((ys, rows, side), BF),
        ),
        in_specs=[SMEM] + [VMEM] * (2 + reps),
        out_specs=(ANY, VMEM),
        scratch_shapes=[pltpu.VMEM((grains, total), BF), pltpu.SemaphoreType.DMA],
        compiler_params=pltpu.CompilerParams(vmem_limit_bytes=VMEM_LIMIT),
        name="dense",
    )(ids, aggs, weight, *others, cot)


def backward_kernel(parts, ids, tiles, mine, theirs, payload, acc):
    acc[...] = jnp.zeros_like(acc)
    side = tiles.shape[1]
    width = acc.shape[1]
    rows = payload.shape[0]
    ys = mine.shape[0]
    col_blocks = acc.shape[0] - 1
    per_row = col_blocks // rows
    base = per_row * width

    slots = tiles.shape[0]
    row_shift = col_blocks.bit_length()
    core_shift = row_shift + per_row.bit_length() - 1
    me = ids[slots]
    for t in range(slots):
        word = ids[t]
        start = ((word >> row_shift) & (per_row - 1)) * width
        block = pl.ds(pl.multiple_of(start, width), width)
        y = (word >> (core_shift + 1)) & (ys - 1)
        local = ((word >> core_shift) & 1) == me
        grad = jnp.where(local, mine[y, block], theirs[y, block])
        acc[word & (2 * col_blocks - 1)] += dot(grad, tiles[t])
    part = (payload.shape[1] - base) // parts
    shares = []
    for k in range(parts):
        half = pl.ds(pl.multiple_of(base + 2 * k * part + me * part, part), part)
        share = jnp.zeros((part, side), F4)
        for grads in (mine, theirs):
            for y in range(ys):
                share += grads[y, half, :].astype(F4)
        shares.append(share.astype(BF))
    for r in range(rows):
        for b in range(per_row):
            payload[r, pl.ds(b * width, width), :] = acc[r * per_row + b].astype(BF)
        for k, share in enumerate(shares):
            payload[r, pl.ds(base + k * part, part), :] = share


def backward_tiles(ids, values, mine, theirs, rows, col_blocks, parts):
    side = values.shape[1]
    base = col_blocks // rows * side
    length = base + (mine.shape[1] - base) // 2
    return pl.pallas_call(
        functools.partial(backward_kernel, parts),
        out_shape=jax.ShapeDtypeStruct((rows, length, side), BF),
        in_specs=[SMEM] + [VMEM] * 3,
        out_specs=VMEM,
        scratch_shapes=[pltpu.VMEM((col_blocks + 1, side, side), F4)],
        compiler_params=pltpu.CompilerParams(vmem_limit_bytes=VMEM_LIMIT),
        name="backward_tiles",
    )(ids, values, mine, theirs)


def finish_kernel(scale, parts, grad, share):
    rows, length, side = parts.shape
    width = side
    grains = grad.shape[0] // rows
    base = grains // side * width
    total = parts[0].astype(F4)
    for r in range(1, rows):
        total += parts[r].astype(F4)
    for b in range(grains // side):
        block = total[b * width : (b + 1) * width].T.astype(BF)
        for r in range(rows):
            grad[pl.ds(r * grains + b * side, side), :] = block
    part = share.shape[0]
    for k in range(share.shape[1] // side):
        share[:, k * side : (k + 1) * side] = total[base + k * part : base + (k + 1) * part] * scale


def finish(parts, scale, grains, part, total):
    rows, length, side = parts.shape
    return pl.pallas_call(
        functools.partial(finish_kernel, scale),
        out_shape=(
            jax.ShapeDtypeStruct((rows * grains, side), BF),
            jax.ShapeDtypeStruct((part, total), F4),
        ),
        in_specs=[VMEM],
        out_specs=(VMEM, VMEM),
        compiler_params=pltpu.CompilerParams(vmem_limit_bytes=VMEM_LIMIT),
        name="finish",
    )(parts)


def place_kernel(chunk_at, steps, ids, *refs):
    pieces, out = refs[:-1], refs[-1]
    part = pieces[0].shape[0]
    for step, piece in zip(steps, pieces):
        start = ((ids[chunk_at] + step) & (len(steps) - 1)) * part
        out[pl.ds(pl.multiple_of(start, part), part), :] = piece[...]


def gather_chunks(ids, chunk_at, piece, holders):
    steps = [0, 1, -1, 2][:holders]
    n = lax.axis_size("y")
    pieces = [piece] + [
        lax.ppermute(piece, "y", [((i + k) % n, i) for i in range(n)]) for k in steps[1:]
    ]
    part, total = piece.shape
    half = pl.pallas_call(
        functools.partial(place_kernel, chunk_at, steps),
        out_shape=jax.ShapeDtypeStruct((part * holders, total), F4),
        in_specs=[SMEM] + [VMEM] * holders,
        out_specs=VMEM,
        compiler_params=pltpu.CompilerParams(vmem_limit_bytes=VMEM_LIMIT),
        name="place",
    )(ids, *pieces)
    return lax.all_gather(half, "core", axis=0, tiled=True)


def around(x, axis, count):
    n = lax.axis_size(axis)
    if count != 4:
        return [
            lax.ppermute(x, axis, [((i + k) % n, i) for i in range(n)]) for k in range(1, count)
        ]
    names, place = (("y", "core"), (2, 1)) if axis == "y" else (("core", axis), (1, n))
    step, core = place
    sides = lax.ppermute(
        x,
        names,
        [
            ((i + k) % n * step + c * core, i * step + c * core)
            for c, k in ((0, 1), (1, -1))
            for i in range(n)
        ],
    )
    across = lax.ppermute(x, axis, [((i + 2) % n, i) for i in range(n)])
    sides = lax.all_gather(sides, "core", axis=0)
    return [sides[0], across, sides[1]]


def swap_cores(x):
    return lax.ppermute(x, "core", [(0, 1), (1, 0)])


def exchange(x, axis):
    return lax.all_to_all(x, axis, 0, 0, tiled=True)


def body(tile_values, tile_rows, tile_cols, tile_count, features, weight, cotangent):
    values = tile_values[0, 0]
    side = values.shape[-1]
    width = features.shape[1]
    grains, total = cotangent.shape
    ys, rows, reps = (lax.axis_size(a) for a in ("y", "row", "rep"))
    col_blocks = features.shape[0] // side
    row_blocks = 2 * ys * grains // side
    nodes = grains * rows * ys * 2
    holders = min(HOLDERS, ys)

    slots = values.shape[0]
    where = [lax.axis_index(a).astype(jnp.int32) for a in ("core", "y", "rep")]
    ids = pack_ids(
        tile_rows[0, 0], tile_cols[0, 0], tile_count[0, 0], row_blocks, col_blocks, *where
    )
    feats = features.reshape(col_blocks, side, width)
    own, other = forward_tiles(ids, values, feats, ys, grains)
    pair = (own + swap_cores(other).astype(F4)).astype(BF)
    pair, lent = lax.optimization_barrier((pair, weight))
    parts = exchange(pair, "y")
    others = around(lent, "rep", reps)
    copies, near, cot = fold(parts, weight, cotangent, reps, others)
    aggs = exchange(copies, "rep")
    activation, payload = dense(ids, aggs, near, others, cot, ys, side)
    mine = exchange(payload, "y")
    theirs = swap_cores(mine)
    back = backward_tiles(ids, values, mine, theirs, rows, col_blocks, total // side)
    sums = exchange(back, "row")
    grad, share = finish(sums, 1.0 / math.sqrt(nodes), grains, width // holders // 2, total)
    input_grad = exchange(grad, "row")
    weight_grad = gather_chunks(ids, slots + 1, share, holders)
    return (activation, weight_grad, input_grad)


def solution(mesh):
    rows, cols, reps = mesh.devices.shape
    split = Mesh(
        mesh.devices.reshape(rows, cols // 2, 2, reps), ("row", "y", "core", "rep")
    )
    col = ("y", "core")
    return jax.shard_map(
        body,
        mesh=split,
        in_specs=(
            P("row", col, None, None, None),
            P("row", col, None),
            P("row", col, None),
            P("row", col),
            P(col, "rep"),
            P("rep", None),
            P(("row",) + col, None),
        ),
        out_specs=(P(("row",) + col, None), P("rep", None), P(col, "rep")),
        check_vma=False,
    )
```

```python
import functools
import math

import jax
import jax.numpy as jnp
from jax import lax
from jax.experimental import pallas as pl
from jax.experimental.pallas import tpu as pltpu
from jax.sharding import Mesh
from jax.sharding import PartitionSpec as P

VMEM_LIMIT = 40 * 1024 * 1024
PIECES = 2
BF = jnp.bfloat16
F4 = jnp.float32

VMEM = pl.BlockSpec(memory_space=pltpu.VMEM)
SMEM = pl.BlockSpec(memory_space=pltpu.SMEM)
ANY = pl.BlockSpec(memory_space=pl.ANY)
HOLDERS = 4


def in_hbm(x):
    return pltpu.with_memory_space_constraint(x, pltpu.HBM)


def dot(a, b, dims=(((1,), (0,)), ((), ()))):
    return lax.dot_general(a, b, dims, preferred_element_type=F4)


def tile_copies(values, tiles, sems):
    piece = tiles.shape[0] // PIECES
    spans = [pl.ds(k * piece, piece) for k in range(PIECES)]
    return [
        pltpu.make_async_copy(values.at[span], tiles.at[span], sems.at[k])
        for k, span in enumerate(spans)
    ]


def pack_ids(row_ids, col_ids, used, row_blocks, col_blocks, *extra):
    slots = row_ids.shape[0]
    at = jnp.arange(slots, dtype=jnp.int32)
    span = 2 * col_blocks
    words = jnp.where(at < used, row_ids * span + col_ids, row_blocks * span + col_blocks)
    at = jnp.arange(slots + len(extra), dtype=jnp.int32)
    words = jnp.pad(words, (0, len(extra)))
    for k, word in enumerate(extra):
        words = jnp.where(at == slots + k, word, words)
    return words


def forward_kernel(ids_any, values, feats_any, own, other, ids, feats, tiles, acc, sems, more_sems):
    first = [
        pltpu.make_async_copy(ids_any, ids, more_sems.at[0]),
        pltpu.make_async_copy(feats_any, feats, more_sems.at[1]),
    ]
    copies = tile_copies(values, tiles, sems)
    for copy in first + copies:
        copy.start()
    acc[...] = jnp.zeros_like(acc)
    for copy in first:
        copy.wait()
    slots = tiles.shape[0]
    col_blocks, side, _ = feats.shape
    row_shift = col_blocks.bit_length()
    piece = slots // PIECES
    for k, copy in enumerate(copies):
        copy.wait()
        for t in range(k * piece, (k + 1) * piece):
            acc[ids[t] >> row_shift] += dot(tiles[t], feats[ids[t] & (col_blocks - 1)])
    ys, grains, _ = own.shape
    blocks = grains // side
    me = ids[slots]
    for y in range(ys):
        for b in range(blocks):
            rows = pl.ds(b * side, side)
            own[y, rows, :] = acc[(2 * y + me) * blocks + b]
            other[y, rows, :] = acc[(2 * y + 1 - me) * blocks + b].astype(BF)


def forward_tiles(ids, values, feats, ys, grains):
    slots, side, _ = values.shape
    width = feats.shape[-1]
    row_blocks = 2 * ys * grains // side
    return pl.pallas_call(
        forward_kernel,
        out_shape=(
            jax.ShapeDtypeStruct((ys, grains, width), F4),
            jax.ShapeDtypeStruct((ys, grains, width), BF),
        ),
        in_specs=[ANY, ANY, ANY],
        out_specs=(VMEM, VMEM),
        scratch_shapes=[
            pltpu.SMEM(ids.shape, jnp.int32),
            pltpu.VMEM(feats.shape, BF),
            pltpu.VMEM((slots, side, side), BF),
            pltpu.VMEM((row_blocks + 1, side, width), F4),
            pltpu.SemaphoreType.DMA((PIECES,)),
            pltpu.SemaphoreType.DMA((2,)),
        ],
        compiler_params=pltpu.CompilerParams(vmem_limit_bytes=VMEM_LIMIT),
        name="forward_tiles",
    )(ids, in_hbm(values), in_hbm(feats))


def fold_kernel(parts_hbm, weight_hbm, cot_hbm, *refs):
    copies, weight, cot, parts, sems, more_sems = refs[-6:]
    bring = [
        pltpu.make_async_copy(parts_hbm.at[y], parts.at[y], sems.at[y])
        for y in range(parts.shape[0])
    ]
    more = [
        pltpu.make_async_copy(weight_hbm, weight, more_sems.at[0]),
        pltpu.make_async_copy(cot_hbm, cot, more_sems.at[1]),
    ]
    for copy in bring + more:
        copy.start()
    bring[0].wait()
    total = parts[0].astype(F4)
    for y in range(1, parts.shape[0]):
        bring[y].wait()
        total += parts[y].astype(F4)
    total = total.astype(BF)
    for q in range(copies.shape[0]):
        copies[q] = total
    for copy in more:
        copy.wait()


def fold(parts, weight, cot, copies, before):
    return pl.pallas_call(
        fold_kernel,
        out_shape=(
            jax.ShapeDtypeStruct((copies,) + parts.shape[1:], BF),
            pltpu.VMEM(weight.shape, BF),
            pltpu.VMEM(cot.shape, BF),
        ),
        in_specs=[ANY] * (3 + len(before)),
        out_specs=(VMEM,) * 3,
        scratch_shapes=[
            pltpu.VMEM(parts.shape, BF),
            pltpu.SemaphoreType.DMA(parts.shape[:1]),
            pltpu.SemaphoreType.DMA((2,)),
        ],
        compiler_params=pltpu.CompilerParams(vmem_limit_bytes=VMEM_LIMIT),
        name="fold",
    )(in_hbm(parts), in_hbm(weight), in_hbm(cot), *before)


def dense_kernel(rep_at, ids, aggs, own_weight, *refs):
    reps, grains, width = aggs.shape
    others, (cot, act_hbm, payload, act, sem) = refs[: reps - 1], refs[reps - 1 :]
    take_act = pltpu.make_async_copy(act, act_hbm, sem)
    me = ids[rep_at]
    ys, _, side = payload.shape
    own_agg = aggs[me]
    hidden = dot(own_agg, own_weight[...])
    for k, weight in enumerate(others):
        hidden += dot(aggs[(me + k + 1) % reps], weight[...])
    sigma = jax.nn.sigmoid(hidden)
    act[...] = (hidden * sigma).astype(BF)
    take_act.start()
    slope = sigma * (1.0 + hidden * (1.0 - sigma))
    grad_hidden = (cot[...].astype(F4) * slope).astype(BF)
    back = dot(own_weight[...], grad_hidden, (((1,), (1,)), ((), ()))).astype(BF)
    share = dot(own_agg, grad_hidden, (((0,), (0,)), ((), ()))).astype(BF)
    holders = min(HOLDERS, ys)
    part = width // holders
    base = grains // side * width
    for y in range(ys):
        for b in range(grains // side):
            payload[y, pl.ds(b * width, width), :] = back[:, b * side : (b + 1) * side]
        chunk = y % holders
        for k in range(share.shape[1] // side):
            payload[y, pl.ds(base + k * part, part), :] = share[
                chunk * part : (chunk + 1) * part, k * side : (k + 1) * side
            ]
    take_act.wait()


def dense(ids, aggs, weight, others, cot, ys, side):
    reps, grains, width = aggs.shape
    total = cot.shape[1]
    rows = grains // side * width + width // min(HOLDERS, ys) * (total // side)
    return pl.pallas_call(
        functools.partial(dense_kernel, ids.shape[0] - 1),
        out_shape=(
            jax.ShapeDtypeStruct((grains, total), BF),
            jax.ShapeDtypeStruct((ys, rows, side), BF),
        ),
        in_specs=[SMEM] + [VMEM] * (2 + reps),
        out_specs=(ANY, VMEM),
        scratch_shapes=[pltpu.VMEM((grains, total), BF), pltpu.SemaphoreType.DMA],
        compiler_params=pltpu.CompilerParams(vmem_limit_bytes=VMEM_LIMIT),
        name="dense",
    )(ids, aggs, weight, *others, cot)


def backward_kernel(parts, ids, tiles, mine, theirs, payload, acc):
    acc[...] = jnp.zeros_like(acc)
    side = tiles.shape[1]
    width = acc.shape[1]
    rows = payload.shape[0]
    ys = mine.shape[0]
    col_blocks = acc.shape[0] - 1
    per_row = col_blocks // rows
    base = per_row * width

    slots = tiles.shape[0]
    row_shift = col_blocks.bit_length()
    core_shift = row_shift + per_row.bit_length() - 1
    me = ids[slots]
    for t in range(slots):
        word = ids[t]
        start = ((word >> row_shift) & (per_row - 1)) * width
        block = pl.ds(pl.multiple_of(start, width), width)
        y = (word >> (core_shift + 1)) & (ys - 1)
        local = ((word >> core_shift) & 1) == me
        grad = jnp.where(local, mine[y, block], theirs[y, block])
        acc[word & (2 * col_blocks - 1)] += dot(grad, tiles[t])
    part = (payload.shape[1] - base) // parts
    shares = []
    for k in range(parts):
        half = pl.ds(pl.multiple_of(base + 2 * k * part + me * part, part), part)
        share = jnp.zeros((part, side), F4)
        for grads in (mine, theirs):
            for y in range(ys):
                share += grads[y, half, :].astype(F4)
        shares.append(share.astype(BF))
    for r in range(rows):
        for b in range(per_row):
            payload[r, pl.ds(b * width, width), :] = acc[r * per_row + b].astype(BF)
        for k, share in enumerate(shares):
            payload[r, pl.ds(base + k * part, part), :] = share


def backward_tiles(ids, values, mine, theirs, rows, col_blocks, parts):
    side = values.shape[1]
    base = col_blocks // rows * side
    length = base + (mine.shape[1] - base) // 2
    return pl.pallas_call(
        functools.partial(backward_kernel, parts),
        out_shape=jax.ShapeDtypeStruct((rows, length, side), BF),
        in_specs=[SMEM] + [VMEM] * 3,
        out_specs=VMEM,
        scratch_shapes=[pltpu.VMEM((col_blocks + 1, side, side), F4)],
        compiler_params=pltpu.CompilerParams(vmem_limit_bytes=VMEM_LIMIT),
        name="backward_tiles",
    )(ids, values, mine, theirs)


def finish_kernel(scale, parts, grad, share):
    rows, length, side = parts.shape
    width = side
    grains = grad.shape[0] // rows
    base = grains // side * width
    total = parts[0].astype(F4)
    for r in range(1, rows):
        total += parts[r].astype(F4)
    for b in range(grains // side):
        block = total[b * width : (b + 1) * width].T.astype(BF)
        for r in range(rows):
            grad[pl.ds(r * grains + b * side, side), :] = block
    part = share.shape[0]
    for k in range(share.shape[1] // side):
        share[:, k * side : (k + 1) * side] = total[base + k * part : base + (k + 1) * part] * scale


def finish(parts, scale, grains, part, total):
    rows, length, side = parts.shape
    return pl.pallas_call(
        functools.partial(finish_kernel, scale),
        out_shape=(
            jax.ShapeDtypeStruct((rows * grains, side), BF),
            jax.ShapeDtypeStruct((part, total), F4),
        ),
        in_specs=[VMEM],
        out_specs=(VMEM, VMEM),
        compiler_params=pltpu.CompilerParams(vmem_limit_bytes=VMEM_LIMIT),
        name="finish",
    )(parts)


def gather_chunks(half, holders):
    groups = [list(range(y, y + holders)) for y in range(0, lax.axis_size("y"), holders)]
    chunk = lax.all_gather(half, "core", axis=0, tiled=True)
    return lax.all_gather(chunk, "y", axis=0, axis_index_groups=groups, tiled=True)


def around(x, axis, count):
    n = lax.axis_size(axis)
    if count != 4:
        return [
            lax.ppermute(x, axis, [((i + k) % n, i) for i in range(n)]) for k in range(1, count)
        ]
    names, place = (("y", "core"), (2, 1)) if axis == "y" else (("core", axis), (1, n))
    step, core = place
    sides = lax.ppermute(
        x,
        names,
        [
            ((i + k) % n * step + c * core, i * step + c * core)
            for c, k in ((0, 1), (1, -1))
            for i in range(n)
        ],
    )
    across = lax.ppermute(x, axis, [((i + 2) % n, i) for i in range(n)])
    sides = lax.all_gather(sides, "core", axis=0)
    return [sides[0], across, sides[1]]


def swap_cores(x):
    return lax.ppermute(x, "core", [(0, 1), (1, 0)])


def exchange(x, axis):
    return lax.all_to_all(x, axis, 0, 0, tiled=True)


def body(tile_values, tile_rows, tile_cols, tile_count, features, weight, cotangent):
    values = tile_values[0, 0]
    side = values.shape[-1]
    width = features.shape[1]
    grains, total = cotangent.shape
    ys, rows, reps = (lax.axis_size(a) for a in ("y", "row", "rep"))
    col_blocks = features.shape[0] // side
    row_blocks = 2 * ys * grains // side
    nodes = grains * rows * ys * 2
    holders = min(HOLDERS, ys)

    slots = values.shape[0]
    where = [lax.axis_index(a).astype(jnp.int32) for a in ("core", "y", "rep")]
    ids = pack_ids(
        tile_rows[0, 0], tile_cols[0, 0], tile_count[0, 0], row_blocks, col_blocks, *where
    )
    feats = features.reshape(col_blocks, side, width)
    own, other = forward_tiles(ids, values, feats, ys, grains)
    pair = (own + swap_cores(other).astype(F4)).astype(BF)
    pair, lent = lax.optimization_barrier((pair, weight))
    parts = exchange(pair, "y")
    others = around(lent, "rep", reps)
    copies, near, cot = fold(parts, weight, cotangent, reps, others)
    aggs = exchange(copies, "rep")
    activation, payload = dense(ids, aggs, near, others, cot, ys, side)
    mine = exchange(payload, "y")
    theirs = swap_cores(mine)
    back = backward_tiles(ids, values, mine, theirs, rows, col_blocks, total // side)
    sums = exchange(back, "row")
    grad, share = finish(sums, 1.0 / math.sqrt(nodes), grains, width // holders // 2, total)
    input_grad = exchange(grad, "row")
    weight_grad = gather_chunks(share, holders)
    return (activation, weight_grad, input_grad)


def solution(mesh):
    rows, cols, reps = mesh.devices.shape
    split = Mesh(
        mesh.devices.reshape(rows, cols // 2, 2, reps), ("row", "y", "core", "rep")
    )
    col = ("y", "core")
    return jax.shard_map(
        body,
        mesh=split,
        in_specs=(
            P("row", col, None, None, None),
            P("row", col, None),
            P("row", col, None),
            P("row", col),
            P(col, "rep"),
            P("rep", None),
            P(("row",) + col, None),
        ),
        out_specs=(P(("row",) + col, None), P("rep", None), P(col, "rep")),
        check_vma=False,
    )
```

```python
import functools
import math

import jax
import jax.numpy as jnp
from jax import lax
from jax.experimental import pallas as pl
from jax.experimental.pallas import tpu as pltpu
from jax.sharding import Mesh
from jax.sharding import PartitionSpec as P

VMEM_LIMIT = 40 * 1024 * 1024
PIECES = 2
BF = jnp.bfloat16
F4 = jnp.float32

VMEM = pl.BlockSpec(memory_space=pltpu.VMEM)
SMEM = pl.BlockSpec(memory_space=pltpu.SMEM)
ANY = pl.BlockSpec(memory_space=pl.ANY)
HOLDERS = 4


def in_hbm(x):
    return pltpu.with_memory_space_constraint(x, pltpu.HBM)


def dot(a, b, dims=(((1,), (0,)), ((), ()))):
    return lax.dot_general(a, b, dims, preferred_element_type=F4)


def tile_copies(values, tiles, sems):
    piece = tiles.shape[0] // PIECES
    spans = [pl.ds(k * piece, piece) for k in range(PIECES)]
    return [
        pltpu.make_async_copy(values.at[span], tiles.at[span], sems.at[k])
        for k, span in enumerate(spans)
    ]


def pack_ids(row_ids, col_ids, used, row_blocks, col_blocks, *extra):
    slots = row_ids.shape[0]
    at = jnp.arange(slots, dtype=jnp.int32)
    span = 2 * col_blocks
    words = jnp.where(at < used, row_ids * span + col_ids, row_blocks * span + col_blocks)
    at = jnp.arange(slots + len(extra), dtype=jnp.int32)
    words = jnp.pad(words, (0, len(extra)))
    for k, word in enumerate(extra):
        words = jnp.where(at == slots + k, word, words)
    return words


def forward_kernel(ids_any, values, feats_any, own, other, ids, feats, tiles, acc, sems, more_sems):
    first = [
        pltpu.make_async_copy(ids_any, ids, more_sems.at[0]),
        pltpu.make_async_copy(feats_any, feats, more_sems.at[1]),
    ]
    copies = tile_copies(values, tiles, sems)
    for copy in first + copies:
        copy.start()
    acc[...] = jnp.zeros_like(acc)
    for copy in first:
        copy.wait()
    slots = tiles.shape[0]
    col_blocks, side, _ = feats.shape
    row_shift = col_blocks.bit_length()
    piece = slots // PIECES
    for k, copy in enumerate(copies):
        copy.wait()
        for t in range(k * piece, (k + 1) * piece):
            acc[ids[t] >> row_shift] += dot(tiles[t], feats[ids[t] & (col_blocks - 1)])
    ys, grains, _ = own.shape
    blocks = grains // side
    me = ids[slots]
    for y in range(ys):
        for b in range(blocks):
            rows = pl.ds(b * side, side)
            own[y, rows, :] = acc[(2 * y + me) * blocks + b]
            other[y, rows, :] = acc[(2 * y + 1 - me) * blocks + b].astype(BF)


def forward_tiles(ids, values, feats, ys, grains):
    slots, side, _ = values.shape
    width = feats.shape[-1]
    row_blocks = 2 * ys * grains // side
    return pl.pallas_call(
        forward_kernel,
        out_shape=(
            jax.ShapeDtypeStruct((ys, grains, width), F4),
            jax.ShapeDtypeStruct((ys, grains, width), BF),
        ),
        in_specs=[ANY, ANY, ANY],
        out_specs=(VMEM, VMEM),
        scratch_shapes=[
            pltpu.SMEM(ids.shape, jnp.int32),
            pltpu.VMEM(feats.shape, BF),
            pltpu.VMEM((slots, side, side), BF),
            pltpu.VMEM((row_blocks + 1, side, width), F4),
            pltpu.SemaphoreType.DMA((PIECES,)),
            pltpu.SemaphoreType.DMA((2,)),
        ],
        compiler_params=pltpu.CompilerParams(vmem_limit_bytes=VMEM_LIMIT),
        name="forward_tiles",
    )(ids, in_hbm(values), in_hbm(feats))


def fold_kernel(parts_hbm, weight_hbm, cot_hbm, *refs):
    copies, weight, cot, parts, sems, more_sems = refs[-6:]
    bring = [
        pltpu.make_async_copy(parts_hbm.at[y], parts.at[y], sems.at[y])
        for y in range(parts.shape[0])
    ]
    more = [
        pltpu.make_async_copy(weight_hbm, weight, more_sems.at[0]),
        pltpu.make_async_copy(cot_hbm, cot, more_sems.at[1]),
    ]
    for copy in bring + more:
        copy.start()
    bring[0].wait()
    total = parts[0].astype(F4)
    for y in range(1, parts.shape[0]):
        bring[y].wait()
        total += parts[y].astype(F4)
    total = total.astype(BF)
    for q in range(copies.shape[0]):
        copies[q] = total
    for copy in more:
        copy.wait()


def fold(parts, weight, cot, copies, before):
    return pl.pallas_call(
        fold_kernel,
        out_shape=(
            jax.ShapeDtypeStruct((copies,) + parts.shape[1:], BF),
            pltpu.VMEM(weight.shape, BF),
            pltpu.VMEM(cot.shape, BF),
        ),
        in_specs=[ANY] * (3 + len(before)),
        out_specs=(VMEM,) * 3,
        scratch_shapes=[
            pltpu.VMEM(parts.shape, BF),
            pltpu.SemaphoreType.DMA(parts.shape[:1]),
            pltpu.SemaphoreType.DMA((2,)),
        ],
        compiler_params=pltpu.CompilerParams(vmem_limit_bytes=VMEM_LIMIT),
        name="fold",
    )(in_hbm(parts), in_hbm(weight), in_hbm(cot), *before)


def dense_kernel(rep_at, ids, aggs, own_weight, *refs):
    reps, grains, width = aggs.shape
    others, (cot, act, payload) = refs[: reps - 1], refs[reps - 1 :]
    me = ids[rep_at]
    ys, _, side = payload.shape
    own_agg = aggs[me]
    near = [own_agg] + [aggs[(me + k) % reps] for k in range(1, reps)]
    weights = [own_weight[...]] + [weight[...] for weight in others]
    hidden = dot(jnp.concatenate(near, axis=1), jnp.concatenate(weights, axis=0))
    sigma = jax.nn.sigmoid(hidden)
    act[...] = (hidden * sigma).astype(BF)
    slope = sigma * (1.0 + hidden * (1.0 - sigma))
    grad_hidden = (cot[...].astype(F4) * slope).astype(BF)
    back = dot(own_weight[...], grad_hidden, (((1,), (1,)), ((), ()))).astype(BF)
    share = dot(own_agg, grad_hidden, (((0,), (0,)), ((), ()))).astype(BF)
    holders = min(HOLDERS, ys)
    part = width // holders
    base = grains // side * width
    for y in range(ys):
        for b in range(grains // side):
            payload[y, pl.ds(b * width, width), :] = back[:, b * side : (b + 1) * side]
        chunk = y % holders
        for k in range(share.shape[1] // side):
            payload[y, pl.ds(base + k * part, part), :] = share[
                chunk * part : (chunk + 1) * part, k * side : (k + 1) * side
            ]


def dense(ids, aggs, weight, others, cot, ys, side):
    reps, grains, width = aggs.shape
    total = cot.shape[1]
    rows = grains // side * width + width // min(HOLDERS, ys) * (total // side)
    return pl.pallas_call(
        functools.partial(dense_kernel, ids.shape[0] - 1),
        out_shape=(
            pltpu.VMEM((grains, total), BF),
            jax.ShapeDtypeStruct((ys, rows, side), BF),
        ),
        in_specs=[SMEM] + [VMEM] * (2 + reps),
        out_specs=(VMEM, VMEM),
        compiler_params=pltpu.CompilerParams(vmem_limit_bytes=VMEM_LIMIT),
        name="dense",
    )(ids, aggs, weight, *others, cot)


def backward_kernel(parts, ids, tiles, mine, theirs, act, payload, act_hbm, acc, sem):
    take_act = pltpu.make_async_copy(act, act_hbm, sem)
    take_act.start()
    acc[...] = jnp.zeros_like(acc)
    side = tiles.shape[1]
    width = acc.shape[1]
    rows = payload.shape[0]
    ys = mine.shape[0]
    col_blocks = acc.shape[0] - 1
    per_row = col_blocks // rows
    base = per_row * width

    slots = tiles.shape[0]
    row_shift = col_blocks.bit_length()
    core_shift = row_shift + per_row.bit_length() - 1
    me = ids[slots]
    for t in range(slots):
        word = ids[t]
        start = ((word >> row_shift) & (per_row - 1)) * width
        block = pl.ds(pl.multiple_of(start, width), width)
        y = (word >> (core_shift + 1)) & (ys - 1)
        local = ((word >> core_shift) & 1) == me
        grad = jnp.where(local, mine[y, block], theirs[y, block])
        acc[word & (2 * col_blocks - 1)] += dot(grad, tiles[t])
    part = (payload.shape[1] - base) // parts
    shares = []
    for k in range(parts):
        half = pl.ds(pl.multiple_of(base + 2 * k * part + me * part, part), part)
        share = jnp.zeros((part, side), F4)
        for grads in (mine, theirs):
            for y in range(ys):
                share += grads[y, half, :].astype(F4)
        shares.append(share.astype(BF))
    for r in range(rows):
        for b in range(per_row):
            payload[r, pl.ds(b * width, width), :] = acc[r * per_row + b].astype(BF)
        for k, share in enumerate(shares):
            payload[r, pl.ds(base + k * part, part), :] = share
    take_act.wait()


def backward_tiles(ids, values, mine, theirs, act, rows, col_blocks, parts):
    side = values.shape[1]
    base = col_blocks // rows * side
    length = base + (mine.shape[1] - base) // 2
    return pl.pallas_call(
        functools.partial(backward_kernel, parts),
        out_shape=(
            jax.ShapeDtypeStruct((rows, length, side), BF),
            jax.ShapeDtypeStruct(act.shape, BF),
        ),
        in_specs=[SMEM] + [VMEM] * 3 + [ANY],
        out_specs=(VMEM, ANY),
        scratch_shapes=[
            pltpu.VMEM((col_blocks + 1, side, side), F4),
            pltpu.SemaphoreType.DMA,
        ],
        compiler_params=pltpu.CompilerParams(vmem_limit_bytes=VMEM_LIMIT),
        name="backward_tiles",
    )(ids, values, mine, theirs, act)


def finish_kernel(scale, parts, grad, share):
    rows, length, side = parts.shape
    width = side
    grains = grad.shape[0] // rows
    base = grains // side * width
    total = parts[0].astype(F4)
    for r in range(1, rows):
        total += parts[r].astype(F4)
    for b in range(grains // side):
        block = total[b * width : (b + 1) * width].T.astype(BF)
        for r in range(rows):
            grad[pl.ds(r * grains + b * side, side), :] = block
    part = share.shape[0]
    for k in range(share.shape[1] // side):
        share[:, k * side : (k + 1) * side] = total[base + k * part : base + (k + 1) * part] * scale


def finish(parts, scale, grains, part, total):
    rows, length, side = parts.shape
    return pl.pallas_call(
        functools.partial(finish_kernel, scale),
        out_shape=(
            jax.ShapeDtypeStruct((rows * grains, side), BF),
            jax.ShapeDtypeStruct((part, total), F4),
        ),
        in_specs=[VMEM],
        out_specs=(VMEM, VMEM),
        compiler_params=pltpu.CompilerParams(vmem_limit_bytes=VMEM_LIMIT),
        name="finish",
    )(parts)


def gather_chunks(half, holders):
    groups = [list(range(y, y + holders)) for y in range(0, lax.axis_size("y"), holders)]
    chunk = lax.all_gather(half, "core", axis=0, tiled=True)
    return lax.all_gather(chunk, "y", axis=0, axis_index_groups=groups, tiled=True)


def around(x, axis, count):
    n = lax.axis_size(axis)
    if count != 4:
        return [
            lax.ppermute(x, axis, [((i + k) % n, i) for i in range(n)]) for k in range(1, count)
        ]
    names, place = (("y", "core"), (2, 1)) if axis == "y" else (("core", axis), (1, n))
    step, core = place
    sides = lax.ppermute(
        x,
        names,
        [
            ((i + k) % n * step + c * core, i * step + c * core)
            for c, k in ((0, 1), (1, -1))
            for i in range(n)
        ],
    )
    across = lax.ppermute(x, axis, [((i + 2) % n, i) for i in range(n)])
    sides = lax.all_gather(sides, "core", axis=0)
    return [sides[0], across, sides[1]]


def swap_cores(x):
    return lax.ppermute(x, "core", [(0, 1), (1, 0)])


def exchange(x, axis):
    return lax.all_to_all(x, axis, 0, 0, tiled=True)


def body(tile_values, tile_rows, tile_cols, tile_count, features, weight, cotangent):
    values = tile_values[0, 0]
    side = values.shape[-1]
    width = features.shape[1]
    grains, total = cotangent.shape
    ys, rows, reps = (lax.axis_size(a) for a in ("y", "row", "rep"))
    col_blocks = features.shape[0] // side
    row_blocks = 2 * ys * grains // side
    nodes = grains * rows * ys * 2
    holders = min(HOLDERS, ys)

    slots = values.shape[0]
    where = [lax.axis_index(a).astype(jnp.int32) for a in ("core", "y", "rep")]
    ids = pack_ids(
        tile_rows[0, 0], tile_cols[0, 0], tile_count[0, 0], row_blocks, col_blocks, *where
    )
    feats = features.reshape(col_blocks, side, width)
    own, other = forward_tiles(ids, values, feats, ys, grains)
    pair = (own + swap_cores(other).astype(F4)).astype(BF)
    pair, lent = lax.optimization_barrier((pair, weight))
    parts = exchange(pair, "y")
    others = around(lent, "rep", reps)
    copies, near, cot = fold(parts, weight, cotangent, reps, others)
    aggs = exchange(copies, "rep")
    act, payload = dense(ids, aggs, near, others, cot, ys, side)
    mine = exchange(payload, "y")
    theirs = swap_cores(mine)
    back, activation = backward_tiles(
        ids, values, mine, theirs, act, rows, col_blocks, total // side
    )
    sums = exchange(back, "row")
    grad, share = finish(sums, 1.0 / math.sqrt(nodes), grains, width // holders // 2, total)
    input_grad = exchange(grad, "row")
    weight_grad = gather_chunks(share, holders)
    return (activation, weight_grad, input_grad)


def solution(mesh):
    rows, cols, reps = mesh.devices.shape
    split = Mesh(
        mesh.devices.reshape(rows, cols // 2, 2, reps), ("row", "y", "core", "rep")
    )
    col = ("y", "core")
    return jax.shard_map(
        body,
        mesh=split,
        in_specs=(
            P("row", col, None, None, None),
            P("row", col, None),
            P("row", col, None),
            P("row", col),
            P(col, "rep"),
            P("rep", None),
            P(("row",) + col, None),
        ),
        out_specs=(P(("row",) + col, None), P("rep", None), P(col, "rep")),
        check_vma=False,
    )
```

```python
import functools
import math

import jax
import jax.numpy as jnp
from jax import lax
from jax.experimental import pallas as pl
from jax.experimental.pallas import tpu as pltpu
from jax.sharding import Mesh
from jax.sharding import PartitionSpec as P

VMEM_LIMIT = 40 * 1024 * 1024
PIECES = 2
BF = jnp.bfloat16
F4 = jnp.float32

VMEM = pl.BlockSpec(memory_space=pltpu.VMEM)
SMEM = pl.BlockSpec(memory_space=pltpu.SMEM)
ANY = pl.BlockSpec(memory_space=pl.ANY)
HOLDERS = 4


def in_hbm(x):
    return pltpu.with_memory_space_constraint(x, pltpu.HBM)


def dot(a, b, dims=(((1,), (0,)), ((), ()))):
    return lax.dot_general(a, b, dims, preferred_element_type=F4)


def tile_copies(values, tiles, sems):
    piece = tiles.shape[0] // PIECES
    spans = [pl.ds(k * piece, piece) for k in range(PIECES)]
    return [
        pltpu.make_async_copy(values.at[span], tiles.at[span], sems.at[k])
        for k, span in enumerate(spans)
    ]


def pack_ids(row_ids, col_ids, used, row_blocks, col_blocks, *extra):
    slots = row_ids.shape[0]
    at = jnp.arange(slots, dtype=jnp.int32)
    span = 2 * col_blocks
    words = jnp.where(at < used, row_ids * span + col_ids, row_blocks * span + col_blocks)
    at = jnp.arange(slots + len(extra), dtype=jnp.int32)
    words = jnp.pad(words, (0, len(extra)))
    for k, word in enumerate(extra):
        words = jnp.where(at == slots + k, word, words)
    return words


def forward_kernel(ids_any, values, feats_any, own, other, ids, feats, tiles, acc, sems, more_sems):
    first = [
        pltpu.make_async_copy(ids_any, ids, more_sems.at[0]),
        pltpu.make_async_copy(feats_any, feats, more_sems.at[1]),
    ]
    copies = tile_copies(values, tiles, sems)
    for copy in first + copies:
        copy.start()
    acc[...] = jnp.zeros_like(acc)
    for copy in first:
        copy.wait()
    slots = tiles.shape[0]
    col_blocks, side, _ = feats.shape
    row_shift = col_blocks.bit_length()
    piece = slots // PIECES
    for k, copy in enumerate(copies):
        copy.wait()
        for t in range(k * piece, (k + 1) * piece):
            acc[ids[t] >> row_shift] += dot(tiles[t], feats[ids[t] & (col_blocks - 1)])
    ys, grains, _ = own.shape
    blocks = grains // side
    me = ids[slots]
    for y in range(ys):
        for b in range(blocks):
            rows = pl.ds(b * side, side)
            own[y, rows, :] = acc[(2 * y + me) * blocks + b]
            other[y, rows, :] = acc[(2 * y + 1 - me) * blocks + b].astype(BF)


def forward_tiles(ids, values, feats, ys, grains):
    slots, side, _ = values.shape
    width = feats.shape[-1]
    row_blocks = 2 * ys * grains // side
    return pl.pallas_call(
        forward_kernel,
        out_shape=(
            jax.ShapeDtypeStruct((ys, grains, width), F4),
            jax.ShapeDtypeStruct((ys, grains, width), BF),
        ),
        in_specs=[ANY, ANY, ANY],
        out_specs=(VMEM, VMEM),
        scratch_shapes=[
            pltpu.SMEM(ids.shape, jnp.int32),
            pltpu.VMEM(feats.shape, BF),
            pltpu.VMEM((slots, side, side), BF),
            pltpu.VMEM((row_blocks + 1, side, width), F4),
            pltpu.SemaphoreType.DMA((PIECES,)),
            pltpu.SemaphoreType.DMA((2,)),
        ],
        compiler_params=pltpu.CompilerParams(vmem_limit_bytes=VMEM_LIMIT),
        name="forward_tiles",
    )(ids, in_hbm(values), in_hbm(feats))


def fold_kernel(parts_hbm, weight_hbm, cot_hbm, *refs):
    copies, weight, cot, parts, sems, more_sems = refs[-6:]
    bring = [
        pltpu.make_async_copy(parts_hbm.at[y], parts.at[y], sems.at[y])
        for y in range(parts.shape[0])
    ]
    more = [
        pltpu.make_async_copy(weight_hbm, weight, more_sems.at[0]),
        pltpu.make_async_copy(cot_hbm, cot, more_sems.at[1]),
    ]
    for copy in bring + more:
        copy.start()
    bring[0].wait()
    total = parts[0].astype(F4)
    for y in range(1, parts.shape[0]):
        bring[y].wait()
        total += parts[y].astype(F4)
    total = total.astype(BF)
    for q in range(copies.shape[0]):
        copies[q] = total
    for copy in more:
        copy.wait()


def fold(parts, weight, cot, copies, before):
    return pl.pallas_call(
        fold_kernel,
        out_shape=(
            jax.ShapeDtypeStruct((copies,) + parts.shape[1:], BF),
            pltpu.VMEM(weight.shape, BF),
            pltpu.VMEM(cot.shape, BF),
        ),
        in_specs=[ANY] * (3 + len(before)),
        out_specs=(VMEM,) * 3,
        scratch_shapes=[
            pltpu.VMEM(parts.shape, BF),
            pltpu.SemaphoreType.DMA(parts.shape[:1]),
            pltpu.SemaphoreType.DMA((2,)),
        ],
        compiler_params=pltpu.CompilerParams(vmem_limit_bytes=VMEM_LIMIT),
        name="fold",
    )(in_hbm(parts), in_hbm(weight), in_hbm(cot), *before)


def dense_kernel(rep_at, ids, aggs, own_weight, *refs):
    reps, grains, width = aggs.shape
    others, (cot, act_hbm, payload, act, sem) = refs[: reps - 1], refs[reps - 1 :]
    take_act = pltpu.make_async_copy(act, act_hbm, sem)
    me = ids[rep_at]
    ys, _, side = payload.shape
    own_agg = aggs[me]
    near = [own_agg] + [aggs[(me + k) % reps] for k in range(1, reps)]
    weights = [own_weight[...]] + [weight[...] for weight in others]
    hidden = dot(jnp.concatenate(near, axis=1), jnp.concatenate(weights, axis=0))
    sigma = jax.nn.sigmoid(hidden)
    act[...] = (hidden * sigma).astype(BF)
    take_act.start()
    slope = sigma * (1.0 + hidden * (1.0 - sigma))
    grad_hidden = (cot[...].astype(F4) * slope).astype(BF)
    back = dot(own_weight[...], grad_hidden, (((1,), (1,)), ((), ()))).astype(BF)
    share = dot(own_agg, grad_hidden, (((0,), (0,)), ((), ()))).astype(BF)
    holders = min(HOLDERS, ys)
    part = width // holders
    base = grains // side * width
    for y in range(ys):
        for b in range(grains // side):
            payload[y, pl.ds(b * width, width), :] = back[:, b * side : (b + 1) * side]
        chunk = y % holders
        for k in range(share.shape[1] // side):
            payload[y, pl.ds(base + k * part, part), :] = share[
                chunk * part : (chunk + 1) * part, k * side : (k + 1) * side
            ]
    take_act.wait()


def dense(ids, aggs, weight, others, cot, ys, side):
    reps, grains, width = aggs.shape
    total = cot.shape[1]
    rows = grains // side * width + width // min(HOLDERS, ys) * (total // side)
    return pl.pallas_call(
        functools.partial(dense_kernel, ids.shape[0] - 1),
        out_shape=(
            jax.ShapeDtypeStruct((grains, total), BF),
            jax.ShapeDtypeStruct((ys, rows, side), BF),
        ),
        in_specs=[SMEM] + [VMEM] * (2 + reps),
        out_specs=(ANY, VMEM),
        scratch_shapes=[pltpu.VMEM((grains, total), BF), pltpu.SemaphoreType.DMA],
        compiler_params=pltpu.CompilerParams(vmem_limit_bytes=VMEM_LIMIT),
        name="dense",
    )(ids, aggs, weight, *others, cot)


def backward_kernel(parts, ids, tiles, mine, theirs, payload, acc):
    acc[...] = jnp.zeros_like(acc)
    side = tiles.shape[1]
    width = acc.shape[1]
    rows = payload.shape[0]
    ys = mine.shape[0]
    col_blocks = acc.shape[0] - 1
    per_row = col_blocks // rows
    base = per_row * width

    slots = tiles.shape[0]
    row_shift = col_blocks.bit_length()
    core_shift = row_shift + per_row.bit_length() - 1
    me = ids[slots]
    for t in range(slots):
        word = ids[t]
        start = ((word >> row_shift) & (per_row - 1)) * width
        block = pl.ds(pl.multiple_of(start, width), width)
        y = (word >> (core_shift + 1)) & (ys - 1)
        local = ((word >> core_shift) & 1) == me
        grad = jnp.where(local, mine[y, block], theirs[y, block])
        acc[word & (2 * col_blocks - 1)] += dot(grad, tiles[t])
    part = (payload.shape[1] - base) // parts
    shares = []
    for k in range(parts):
        half = pl.ds(pl.multiple_of(base + 2 * k * part + me * part, part), part)
        share = jnp.zeros((part, side), F4)
        for grads in (mine, theirs):
            for y in range(ys):
                share += grads[y, half, :].astype(F4)
        shares.append(share.astype(BF))
    for r in range(rows):
        for b in range(per_row):
            payload[r, pl.ds(b * width, width), :] = acc[r * per_row + b].astype(BF)
        for k, share in enumerate(shares):
            payload[r, pl.ds(base + k * part, part), :] = share


def backward_tiles(ids, values, mine, theirs, rows, col_blocks, parts):
    side = values.shape[1]
    base = col_blocks // rows * side
    length = base + (mine.shape[1] - base) // 2
    return pl.pallas_call(
        functools.partial(backward_kernel, parts),
        out_shape=jax.ShapeDtypeStruct((rows, length, side), BF),
        in_specs=[SMEM] + [VMEM] * 3,
        out_specs=VMEM,
        scratch_shapes=[pltpu.VMEM((col_blocks + 1, side, side), F4)],
        compiler_params=pltpu.CompilerParams(vmem_limit_bytes=VMEM_LIMIT),
        name="backward_tiles",
    )(ids, values, mine, theirs)


def finish_kernel(scale, parts, grad, share):
    rows, length, side = parts.shape
    width = side
    grains = grad.shape[0] // rows
    base = grains // side * width
    total = parts[0].astype(F4)
    for r in range(1, rows):
        total += parts[r].astype(F4)
    for b in range(grains // side):
        block = total[b * width : (b + 1) * width].T.astype(BF)
        for r in range(rows):
            grad[pl.ds(r * grains + b * side, side), :] = block
    part = share.shape[0]
    for k in range(share.shape[1] // side):
        share[:, k * side : (k + 1) * side] = total[base + k * part : base + (k + 1) * part] * scale


def finish(parts, scale, grains, part, total):
    rows, length, side = parts.shape
    return pl.pallas_call(
        functools.partial(finish_kernel, scale),
        out_shape=(
            jax.ShapeDtypeStruct((rows * grains, side), BF),
            jax.ShapeDtypeStruct((part, total), F4),
        ),
        in_specs=[VMEM],
        out_specs=(VMEM, VMEM),
        compiler_params=pltpu.CompilerParams(vmem_limit_bytes=VMEM_LIMIT),
        name="finish",
    )(parts)


def gather_chunks(half, holders):
    groups = [list(range(y, y + holders)) for y in range(0, lax.axis_size("y"), holders)]
    chunk = lax.all_gather(half, "core", axis=0, tiled=True)
    return lax.all_gather(chunk, "y", axis=0, axis_index_groups=groups, tiled=True)


def around(x, axis, count):
    n = lax.axis_size(axis)
    if count != 4:
        return [
            lax.ppermute(x, axis, [((i + k) % n, i) for i in range(n)]) for k in range(1, count)
        ]
    names, place = (("y", "core"), (2, 1)) if axis == "y" else (("core", axis), (1, n))
    step, core = place
    sides = lax.ppermute(
        x,
        names,
        [
            ((i + k) % n * step + c * core, i * step + c * core)
            for c, k in ((0, 1), (1, -1))
            for i in range(n)
        ],
    )
    across = lax.ppermute(x, axis, [((i + 2) % n, i) for i in range(n)])
    sides = lax.all_gather(sides, "core", axis=0)
    return [sides[0], across, sides[1]]


def swap_cores(x):
    return lax.ppermute(x, "core", [(0, 1), (1, 0)])


def exchange(x, axis):
    return lax.all_to_all(x, axis, 0, 0, tiled=True)


def body(tile_values, tile_rows, tile_cols, tile_count, features, weight, cotangent):
    values = tile_values[0, 0]
    side = values.shape[-1]
    width = features.shape[1]
    grains, total = cotangent.shape
    ys, rows, reps = (lax.axis_size(a) for a in ("y", "row", "rep"))
    col_blocks = features.shape[0] // side
    row_blocks = 2 * ys * grains // side
    nodes = grains * rows * ys * 2
    holders = min(HOLDERS, ys)

    slots = values.shape[0]
    where = [lax.axis_index(a).astype(jnp.int32) for a in ("core", "y", "rep")]
    ids = pack_ids(
        tile_rows[0, 0], tile_cols[0, 0], tile_count[0, 0], row_blocks, col_blocks, *where
    )
    feats = features.reshape(col_blocks, side, width)
    own, other = forward_tiles(ids, values, feats, ys, grains)
    pair = (own + swap_cores(other).astype(F4)).astype(BF)
    pair, lent = lax.optimization_barrier((pair, weight))
    parts = exchange(pair, "y")
    others = around(lent, "rep", reps)
    copies, near, cot = fold(parts, weight, cotangent, reps, others)
    aggs = exchange(copies, "rep")
    activation, payload = dense(ids, aggs, near, others, cot, ys, side)
    mine = exchange(payload, "y")
    theirs = swap_cores(mine)
    back = backward_tiles(ids, values, mine, theirs, rows, col_blocks, total // side)
    sums = exchange(back, "row")
    grad, share = finish(sums, 1.0 / math.sqrt(nodes), grains, width // holders // 2, total)
    input_grad = exchange(grad, "row")
    weight_grad = gather_chunks(share, holders)
    return (activation, weight_grad, input_grad)


def solution(mesh):
    rows, cols, reps = mesh.devices.shape
    split = Mesh(
        mesh.devices.reshape(rows, cols // 2, 2, reps), ("row", "y", "core", "rep")
    )
    col = ("y", "core")
    return jax.shard_map(
        body,
        mesh=split,
        in_specs=(
            P("row", col, None, None, None),
            P("row", col, None),
            P("row", col, None),
            P("row", col),
            P(col, "rep"),
            P("rep", None),
            P(("row",) + col, None),
        ),
        out_specs=(P(("row",) + col, None), P("rep", None), P(col, "rep")),
        check_vma=False,
    )
```
